32 devices in a mesh: section: 2 (over core), seq: 4 (over z), head: 4 (over y, x).
Axes of the slice: x: 2, y: 2, z: 4, core: 2. Of those that a mesh axis runs over, the one named last changes fastest.
Arguments:
- inputs: bfloat16 [2, 1024, 1024], P(None, 'seq'), may hold values from -6 to 6
- cotangent: bfloat16 [2, 1024, 1024], P(None, 'seq'), may hold values from -6 to 6
- in_gain: float32 [2, 1024], P('section'), may hold values from 0.5 to 1.5
- w_z: bfloat16 [2, 1024, 2048], P('section', None, 'head'), may hold values from -0.1875 to 0.1875
- w_x: bfloat16 [2, 1024, 2048], P('section', None, 'head'), may hold values from -0.1875 to 0.1875
- w_bc: bfloat16 [2, 1024, 2, 128], P('section', None, None, 'head'), may hold values from -0.046875 to 0.046875
- w_dt: bfloat16 [2, 1024, 32], P('section', None, 'head'), may hold values from -0.1875 to 0.1875
- dt_bias: float32 [2, 32], P('section', 'head'), may hold values from -3 to 0
- a_log: float32 [2, 32], P('section', 'head'), may hold values from -9 to -1
- skip: float32 [2, 32], P('section', 'head'), may hold values from 0.5 to 1.5
- conv_x: float32 [2, 4, 2048], P('section', None, 'head'), may hold values from -3 to 3
- conv_bc: float32 [2, 4, 2, 128], P('section', None, None, 'head'), may hold values from -3 to 3
- convb_x: float32 [2, 2048], P('section', 'head'), may hold values from -1.8 to 1.8
- convb_bc: float32 [2, 2, 128], P('section', None, 'head'), may hold values from -0.6 to 0.6
- norm_gain: float32 [2, 2048], P('section', 'head'), may hold values from 0.5 to 1.5
- w_out: bfloat16 [2, 2048, 1024], P('section', 'head'), may hold values from -0.125 to 0.125
Outputs:
- ends: float32 [2, 2, 1024, 1024], P('section', None, 'seq')
- g_in_gain: float32 [2, 1024], P('section')
- g_w_z: float32 [2, 1024, 2048], P('section', 'seq', 'head')
- g_w_x: float32 [2, 1024, 2048], P('section', 'seq', 'head')
- g_w_bc: float32 [2, 1024, 2, 128], P('section', 'seq', None, 'head')
- g_w_dt: float32 [2, 1024, 32], P('section', 'seq', 'head')
- g_dt_bias: float32 [2, 32], P('section', 'head')
- g_a_log: float32 [2, 32], P('section', 'head')
- g_skip: float32 [2, 32], P('section', 'head')
- g_conv_x: float32 [2, 4, 2048], P('section', None, 'head')
- g_conv_bc: float32 [2, 4, 2, 128], P('section', None, None, 'head')
- g_convb_x: float32 [2, 2048], P('section', 'head')
- g_convb_bc: float32 [2, 2, 128], P('section', None, 'head')
- g_norm_gain: float32 [2, 2048], P('section', 'head')
- g_w_out: float32 [2, 2048, 1024], P('section', 'head', 'seq')
The draws below stay inside these ranges and needn't reach their ends.
All inputs are finite; a program needn't handle non-finite values.
Results may differ from the reference program's by a relative error of at most 0.014.
The reference program's roundings to bfloat16 on the way count: a program that leaves them out, or rounds other values in their place, can miss the bound.
Values sent between devices are 32-bit elements; how exact they have to be, the bound alone decides.
No kernel may reach another device: no remote copies, remote signals or barrier semaphores. Data moves between devices by JAX's collectives and lax.ppermute only.
A program may use at most 128 MiB of HBM per device.

```python
from functools import partial
import jax
import jax.numpy as jnp
from jax import lax

D = 1024
ED = 2048
HEAD = 64
N = 128
CONV = 4
STRETCH = 128
MB = 2
H = 32
SEQLEN = 1024
LAYERS = 2


def block_scale(key, dims, cuts, low, largest):
    def one(axis_at, shards_of):
        steps = jax.random.uniform(jax.random.fold_in(jax.random.fold_in(key, 6), axis_at), (shards_of,), jnp.float32, low / len(cuts), largest / len(cuts))
        return jnp.repeat(jnp.exp(steps), dims[axis_at] // shards_of).reshape((-1,) + (1,) * (len(dims) - axis_at - 1))

    loudness = one(*cuts[0])
    for cut in cuts[1:]:
        loudness = loudness * one(*cut)
    return loudness


def centred(own_key, shape, deviation, bound, shards=(), held_as=jnp.bfloat16):
    level = block_scale(own_key, shape, shards, -0.22, 0.18) if shards else 1.0
    drawn = jax.random.normal(own_key, shape, jnp.float32) * deviation * level
    return jnp.minimum(jnp.maximum(drawn, -bound), bound).astype(held_as)


def setup_inputs(seed: int = 0) -> dict:
    arg_keys = jax.random.split(jax.random.key(seed), 17)
    inputs = centred(arg_keys[0], (MB, SEQLEN, D), 1.0, 6.0, ((1, 4),))
    cotangent = centred(arg_keys[1], (MB, SEQLEN, D), 1.0, 6.0, ((1, 4),))
    in_gain = jnp.clip(1.0 + 0.1 * jax.random.normal(arg_keys[2], (LAYERS, D), jnp.float32), 0.5, 1.5)
    w_z = centred(arg_keys[3], (LAYERS, D, ED), D ** -0.5, 0.1875, ((0, 2), (2, 4)))
    w_x = centred(arg_keys[4], (LAYERS, D, ED), D ** -0.5, 0.1875, ((0, 2), (2, 4)))
    w_bc = centred(arg_keys[5], (LAYERS, D, 2, N), (16 * D) ** -0.5, 0.046875, ((0, 2), (3, 4)))
    w_dt = centred(arg_keys[6], (LAYERS, D, H), D ** -0.5, 0.1875, ((0, 2), (2, 4)))
    dt_bias = jnp.clip(-3.0 + 3.0 * jax.random.uniform(arg_keys[7], (LAYERS, H), jnp.float32) ** block_scale(arg_keys[7], (LAYERS, H), ((0, 2), (1, 4)), -0.2, 0.2), -3.0, 0.0)
    a_log = jnp.clip(-9.0 + 8.0 * jax.random.uniform(arg_keys[8], (LAYERS, H), jnp.float32) ** block_scale(arg_keys[8], (LAYERS, H), ((0, 2), (1, 4)), -0.2, 0.2), -9.0, -1.0)
    skip = jnp.clip(0.5 + 1.0 * jax.random.uniform(arg_keys[9], (LAYERS, H), jnp.float32) ** block_scale(arg_keys[9], (LAYERS, H), ((0, 2), (1, 4)), -0.2, 0.2), 0.5, 1.5)
    conv_x = centred(arg_keys[10], (LAYERS, CONV, ED), CONV ** -0.5, 3.0, ((0, 2), (2, 4)), jnp.float32)
    conv_bc = centred(arg_keys[11], (LAYERS, CONV, 2, N), CONV ** -0.5, 3.0, ((0, 2), (3, 4)), jnp.float32)
    convb_x = centred(arg_keys[12], (LAYERS, ED), 0.3, 1.8, ((0, 2), (1, 4)), jnp.float32)
    convb_bc = centred(arg_keys[13], (LAYERS, 2, N), 0.1, 0.6, ((0, 2), (2, 4)), jnp.float32)
    norm_gain = jnp.clip(1.0 + 0.1 * jax.random.normal(arg_keys[14], (LAYERS, ED), jnp.float32), 0.5, 1.5)
    w_out = centred(arg_keys[15], (LAYERS, ED, D), ED ** -0.5, 0.125, ((0, 2), (1, 4)))
    return {"inputs": inputs, "cotangent": cotangent, "in_gain": in_gain, "w_z": w_z, "w_x": w_x, "w_bc": w_bc, "w_dt": w_dt, "dt_bias": dt_bias, "a_log": a_log, "skip": skip, "conv_x": conv_x, "conv_bc": conv_bc, "convb_x": convb_x, "convb_bc": convb_bc, "norm_gain": norm_gain, "w_out": w_out}


EPS = 1e-05
HIGH = lax.Precision.HIGHEST

@jax.custom_vjp
def low(v):
    return lax.optimization_barrier(v.astype(jnp.bfloat16)).astype(jnp.float32)

@jax.custom_vjp
def low_back(v):
    return v

def low_keep(v):
    return (low(v), None)

def low_pass(kept, grad):
    return (grad,)

def back_keep(v):
    return (v, None)

def back_low(kept, grad):
    return (low(grad),)
low.defvjp(low_keep, low_pass)
low_back.defvjp(back_keep, back_low)

def matmul_hi(left, right):
    return jnp.dot(left, right, precision=HIGH, preferred_element_type=jnp.float32)

def rms_scale(values):
    return lax.rsqrt(lax.optimization_barrier(jnp.mean(values * values, axis=-1, keepdims=True)) + EPS)

def stretch_step(log_rate, ssm_state, pieces):
    x_stretch, b_stretch, c_stretch, step_stretch = pieces
    stretch_len = x_stretch.shape[0]
    log_cum = jnp.cumsum(step_stretch * log_rate[None, :], axis=0)
    lower_mask = jnp.arange(stretch_len)[:, None] >= jnp.arange(stretch_len)[None, :]
    log_gap = log_cum[:, None, :] - log_cum[None, :, :]
    decay_mat = jnp.where(lower_mask[:, :, None], jnp.exp(jnp.minimum(log_gap, 0.0)), 0.0)
    inner_prod = matmul_hi(c_stretch, b_stretch.T)
    mix_weights = inner_prod[:, :, None] * decay_mat * step_stretch[None, :, :]
    stretch_out = jnp.einsum('qkh,khp->qhp', mix_weights, x_stretch, precision=HIGH)
    stretch_out = stretch_out + jnp.exp(log_cum)[:, :, None] * jnp.einsum('qn,hpn->qhp', c_stretch, ssm_state, precision=HIGH)
    tail_w = jnp.exp(log_cum[-1][None, :] - log_cum) * step_stretch
    new_state = jnp.exp(log_cum[-1])[:, None, None] * ssm_state + jnp.einsum('kh,khp,kn->hpn', tail_w, x_stretch, b_stretch, precision=HIGH)
    return (new_state, stretch_out)

def mamba_block(resid, in_gain, w_z, w_x, w_bc, w_dt, dt_bias, a_log, skip, conv_x, conv_bc, convb_x, convb_bc, norm_gain, w_out):
    seq_len, model_w = resid.shape
    inner_w = w_z.shape[1]
    state_w = w_bc.shape[2]
    n_heads = w_dt.shape[1]
    normed = low(resid * rms_scale(resid) * in_gain[None, :])
    gate_in = low_back(matmul_hi(normed, w_z))
    x_in = low_back(matmul_hi(normed, w_x))
    bc_in = low_back(matmul_hi(normed, w_bc.reshape(model_w, 2 * state_w)))
    dt_in = low_back(matmul_hi(normed, w_dt))
    mixed_in = jnp.concatenate([x_in, bc_in], axis=1)
    kernel = jnp.concatenate([conv_x, conv_bc.reshape(CONV, 2 * state_w)], axis=1)
    shift_b = jnp.concatenate([convb_x, convb_bc.reshape(2 * state_w)])
    padded = jnp.concatenate([jnp.zeros((CONV - 1, mixed_in.shape[1]), jnp.float32), mixed_in], axis=0)
    conv_out = shift_b[None, :] + sum((kernel[tap][None, :] * padded[tap:tap + seq_len] for tap in range(CONV)))
    activated = jax.nn.silu(conv_out)
    x_ssd = activated[:, :inner_w].reshape(seq_len, n_heads, HEAD)
    b_ssd = activated[:, inner_w:inner_w + state_w]
    c_ssd = activated[:, inner_w + state_w:]
    step_size = jax.nn.softplus(dt_in + dt_bias[None, :])
    log_rate = -jnp.exp(a_log)
    n_stretches = seq_len // STRETCH
    pieces = (x_ssd.reshape(n_stretches, STRETCH, n_heads, HEAD), b_ssd.reshape(n_stretches, STRETCH, state_w), c_ssd.reshape(n_stretches, STRETCH, state_w), step_size.reshape(n_stretches, STRETCH, n_heads))
    zero_state = jnp.zeros((n_heads, HEAD, state_w), jnp.float32)
    last_state, stretch_outs = lax.scan(jax.checkpoint(partial(stretch_step, log_rate)), zero_state, pieces)
    ssd_out = stretch_outs.reshape(seq_len, n_heads, HEAD) + skip[None, :, None] * x_ssd
    ssd_flat = ssd_out.reshape(seq_len, inner_w)
    gated_out = ssd_flat * jax.nn.silu(gate_in)
    norm_out = low(gated_out * rms_scale(gated_out) * norm_gain[None, :])
    branch = low_back(matmul_hi(norm_out, w_out))
    return resid + branch

def reference(inputs, cotangent, in_gain, w_z, w_x, w_bc, w_dt, dt_bias, a_log, skip, conv_x, conv_bc, convb_x, convb_bc, norm_gain, w_out):
    params = tuple((weight.astype(jnp.float32) for weight in (in_gain, w_z, w_x, w_bc, w_dt, dt_bias, a_log, skip, conv_x, conv_bc, convb_x, convb_bc, norm_gain, w_out)))

    def both_sections(weights, block_in):
        hidden = mamba_block(block_in, *[weight[0] for weight in weights])
        return mamba_block(hidden, *[weight[1] for weight in weights])

    def per_batch(totals, mb_pair):
        block_in, cotan_mb = mb_pair
        result, pullback = jax.vjp(both_sections, params, block_in)
        grad_sums, in_grad = pullback(cotan_mb)
        return (tuple((total + grad for total, grad in zip(totals, grad_sums))), (result, in_grad))
    zero_grads = tuple((jnp.zeros_like(weight) for weight in params))
    totals, outputs = lax.scan(per_batch, zero_grads, (inputs.astype(jnp.float32), cotangent.astype(jnp.float32)))
    results, in_grads = outputs
    ends = jnp.stack([in_grads, results])
    return (ends, totals[0], totals[1], totals[2], totals[3], totals[4], totals[5], totals[6], totals[7], totals[8], totals[9], totals[10], totals[11], totals[12], totals[13])
```

```python
import functools

import jax
import jax.numpy as jnp
from jax import lax
from jax.experimental import pallas as pl
from jax.experimental.pallas import tpu as pltpu
from jax.sharding import PartitionSpec as P

ED = 2048
HEAD = 64
CONV = 4
EPS = 1e-05
EDGE = 8
LANES = 128
F32 = jnp.float32
BF16 = jnp.bfloat16
NN = (((1,), (0,)), ((), ()))
NT = (((1,), (1,)), ((), ()))
TN = (((0,), (0,)), ((), ()))


def dot_low(left, right, dims=NN):
    return lax.dot_general(left.astype(BF16), right.astype(BF16), dims, preferred_element_type=F32)


def halves(value):
    high = value.astype(BF16)
    return high, (value - high.astype(F32)).astype(BF16)


def dot_split(left, right, dims=NN):
    left_hi, left_lo = halves(left)
    right_hi, right_lo = halves(right)
    mul = functools.partial(lax.dot_general, dimension_numbers=dims, preferred_element_type=F32)
    return mul(left_hi, right_hi) + (mul(left_hi, right_lo) + mul(left_lo, right_hi))


def dot_exact(left, right, dims=NN):
    return lax.dot_general(
        left, right, dims, precision=lax.Precision.HIGHEST, preferred_element_type=F32
    )


dot_mix = dot_split
dot_sum = dot_exact


def kernel_call(body, outs, args, time_us, scratch=(), scalars=True):
    specs = [pl.BlockSpec(memory_space=pltpu.VMEM)] * len(args)
    if scalars:
        specs[0] = pl.BlockSpec(memory_space=pltpu.SMEM)
    return pl.pallas_call(
        body,
        out_shape=[jax.ShapeDtypeStruct(shape, dtype) for shape, dtype in outs],
        in_specs=specs,
        out_specs=[pl.BlockSpec(memory_space=pltpu.VMEM)] * len(outs),
        scratch_shapes=list(scratch),
        compiler_params=pltpu.CompilerParams(vmem_limit_bytes=40 * 1024 * 1024),
        cost_estimate=pl.CostEstimate(
            flops=0, bytes_accessed=int(time_us * 3_000_000), transcendentals=0
        ),
    )(*args)


def sigmoid(values):
    return 1.0 / (1.0 + jnp.exp(-values))


def softplus(values):
    return jnp.maximum(values, 0.0) + jnp.log1p(jnp.exp(-jnp.abs(values)))


def one_hot(channels):
    head_of = lax.broadcasted_iota(jnp.int32, (channels, LANES), 0) // HEAD
    return (head_of == lax.broadcasted_iota(jnp.int32, (channels, LANES), 1)).astype(F32)


def spread(per_head, channels):
    rows = per_head.shape[0]
    return jnp.concatenate(
        [
            jnp.broadcast_to(per_head[:, head : head + 1], (rows, HEAD))
            for head in range(channels // HEAD)
        ],
        axis=1,
    )


def ordered(tokens):
    row = lax.broadcasted_iota(jnp.int32, (tokens, tokens), 0)
    col = lax.broadcasted_iota(jnp.int32, (tokens, tokens), 1)
    return row >= col


def place(scalars_ref, half, part, parts, rows):
    section = scalars_ref[0]
    head = scalars_ref[1]
    side = section if half == 0 else 1 - section
    start = (side * parts + jnp.bitwise_xor(head, part)) * rows
    return pl.multiple_of(start, rows)


def gather_rows(scalars_ref, target_ref, own_ref, other_ref, parts):
    rows = own_ref.shape[0] // parts
    for half, source in enumerate((own_ref, other_ref)):
        for part in range(parts):
            start = place(scalars_ref, half, part, parts, rows)
            target_ref[pl.ds(start, rows), :] = source[part * rows : (part + 1) * rows, :]


def deal_rows(scalars_ref, source_ref, keep_ref, send_ref, parts):
    rows = keep_ref.shape[0] // parts
    for half, target in enumerate((keep_ref, send_ref)):
        for part in range(parts):
            start = place(scalars_ref, half, part, parts, rows)
            target[part * rows : (part + 1) * rows, :] = source_ref[pl.ds(start, rows), :]


def pick_weights(
    where_ref, z_ref, x_ref, out_ref, got_zx_ref, got_out_ref, own_pack_ref, other_pack_ref,
    zx0_ref, zx1_ref, bc0_ref, bc1_ref, dt0_ref, dt1_ref, out0_ref, out1_ref, *, heads_n
):
    section = where_ref[0]
    model_w = z_ref.shape[0]
    inner = zx0_ref.shape[1] // 2
    channels = bc0_ref.shape[1]
    here = pl.ds(pl.multiple_of(section * inner, inner), inner)
    lane = lax.broadcasted_iota(jnp.int32, (model_w, LANES), 1)

    def narrow(pack_ref):
        both = pack_ref[:model_w, channels:]
        side = jnp.where(section == 0, both, pltpu.roll(both, LANES - heads_n, 1))
        return jnp.where(lane < heads_n, side, 0.0).astype(BF16)

    own = (z_ref[:, here], x_ref[:, here])
    got = (got_zx_ref[:, :inner].astype(BF16), got_zx_ref[:, inner:].astype(BF16))
    own_out = out_ref[here, :]
    got_out = got_out_ref[...].astype(BF16)
    own_bc = own_pack_ref[:model_w, :channels].astype(BF16)
    other_bc = other_pack_ref[:model_w, :channels].astype(BF16)
    own_dt = narrow(own_pack_ref)
    other_dt = narrow(other_pack_ref)

    def write(first, second):
        for source, refs in (
            (first, (zx0_ref, bc0_ref, dt0_ref, out0_ref)),
            (second, (zx1_ref, bc1_ref, dt1_ref, out1_ref)),
        ):
            zx_from, bc_from, dt_from, out_from = source
            refs[0][:, :inner] = zx_from[0]
            refs[0][:, inner:] = zx_from[1]
            refs[1][...] = bc_from
            refs[2][...] = dt_from
            refs[3][...] = out_from

    own_set = (own, own_bc, own_dt, own_out)
    got_set = (got, other_bc, other_dt, got_out)

    @pl.when(section == 0)
    def _():
        write(own_set, got_set)

    @pl.when(section != 0)
    def _():
        write(got_set, own_set)


def project(block_in, halo, in_gain, w_zx, w_bc, w_dt, taps, heads, outs):
    normed_ref, gate_ref, pad_ref, conv_ref, dt_ref, cum_ref, local_ref, state_ref = outs
    tokens = block_in.shape[0]
    inner = w_zx.shape[1] // 2
    rows = jnp.concatenate([halo, block_in], axis=0)
    scale = lax.rsqrt(jnp.mean(rows * rows, axis=-1, keepdims=True) + EPS)
    normed = (rows * scale * in_gain).astype(BF16)
    low = normed[EDGE:]
    normed_ref[...] = low
    gate_ref[...] = dot_low(low, w_zx[:, :inner])
    pad_ref[:, :inner] = dot_low(normed, w_zx[:, inner:])
    pad_ref[:, inner:] = dot_low(normed, w_bc)
    dt_val = dot_low(low, w_dt) + heads[0:1, :]
    dt_ref[...] = dt_val
    conv = taps[CONV : CONV + 1, :]
    for tap in range(CONV):
        first = EDGE - CONV + 1 + tap
        conv = conv + taps[tap : tap + 1, :] * pad_ref[first : first + tokens, :]
    conv_ref[...] = conv
    act = conv * sigmoid(conv)
    state_w = (act.shape[1] - inner) // 2
    x_ssd = act[:, :inner]
    b_ssd = act[:, inner : inner + state_w]
    c_ssd = act[:, inner + state_w :]
    log_rate = -jnp.exp(heads[1:2, :])
    step = softplus(dt_val)
    lower = ordered(tokens)
    cum = dot_sum(lower.astype(F32), step * log_rate)
    cum_ref[...] = cum
    cum_rows = cum.T
    scaled = x_ssd * spread(step, inner)
    cross = jnp.where(lower, dot_mix(c_ssd, b_ssd, NT), 0.0)
    outputs = []
    for head in range(inner // HEAD):
        gap = cum[:, head : head + 1] - cum_rows[head : head + 1, :]
        mix = cross * jnp.exp(jnp.minimum(gap, 0.0))
        outputs.append(dot_mix(mix, scaled[:, head * HEAD : (head + 1) * HEAD]))
    local_ref[...] = jnp.concatenate(outputs, axis=1) + spread(heads[2:3, :], inner) * x_ssd
    cum_chan = spread(cum, inner)
    last = cum_chan[tokens - 1 : tokens, :]
    state_ref[:state_w, :] = dot_mix(b_ssd, scaled * jnp.exp(last - cum_chan), TN)
    state_ref[state_w:, :] = jnp.broadcast_to(last, (EDGE, inner))


def first_forward(in_ref, halo_ref, gain_ref, zx_ref, bc_ref, dt_ref, taps_ref, heads_ref, *outs):
    project(
        in_ref[...].astype(F32), halo_ref[...], gain_ref[...], zx_ref[...], bc_ref[...],
        dt_ref[...], taps_ref[...], heads_ref[...], outs,
    )


def later_forward(
    parts, where_ref, own_ref, other_ref, halo_ref, gain_ref, zx_ref, bc_ref, dt_ref, taps_ref,
    heads_ref, in_ref, *outs
):
    gather_rows(where_ref, in_ref, own_ref, other_ref, parts)
    project(
        in_ref[...], halo_ref[...], gain_ref[...], zx_ref[...], bc_ref[...], dt_ref[...],
        taps_ref[...], heads_ref[...], outs,
    )


def mixed_output(local_ref, entry_ref, conv_ref, cum_ref, gate_ref):
    inner = local_ref.shape[1]
    state_w = entry_ref.shape[0] - EDGE
    conv_c = conv_ref[:, inner + state_w :]
    c_ssd = conv_c * sigmoid(conv_c)
    grown = jnp.exp(spread(cum_ref[...], inner))
    ssd = local_ref[...] + grown * dot_mix(c_ssd, entry_ref[:state_w, :])
    gate = gate_ref[...]
    return ssd, ssd * (gate * sigmoid(gate))


def sums_of(squares, inner_prod):
    lane = lax.broadcasted_iota(jnp.int32, (squares.shape[0], LANES), 1)
    both = jnp.where(lane == 0, squares, jnp.where(lane == 1, inner_prod, 0.0))
    return both.T[:EDGE, :]


def rate_of(sums):
    fill = jnp.zeros((LANES - sums.shape[0], sums.shape[1]), F32)
    columns = jnp.concatenate([sums, fill], axis=0).T
    return lax.rsqrt(columns[:, :1] / ED + EPS), columns[:, 1:2]


def first_output(local_ref, entry_ref, conv_ref, cum_ref, gate_ref, ssd_ref, sums_ref):
    ssd, gated = mixed_output(local_ref, entry_ref, conv_ref, cum_ref, gate_ref)
    ssd_ref[...] = ssd
    sums_ref[...] = sums_of(jnp.sum(gated * gated, axis=-1, keepdims=True), 0.0)


def first_branch(
    parts, where_ref, sums_ref, ssd_ref, gate_ref, gain_ref, w_out_ref, norm_ref, keep_ref,
    send_ref, whole_ref
):
    rate, _ = rate_of(sums_ref[...])
    gate = gate_ref[...]
    norm_out = (ssd_ref[...] * (gate * sigmoid(gate)) * rate * gain_ref[...]).astype(BF16)
    norm_ref[...] = norm_out
    whole_ref[...] = dot_low(norm_out, w_out_ref[...])
    deal_rows(where_ref, whole_ref, keep_ref, send_ref, parts)


def second_output(
    local_ref, entry_ref, conv_ref, cum_ref, gate_ref, gain_ref, w_out_ref, cot_ref,
    ssd_ref, grad_norm_ref, sums_ref
):
    ssd, gated = mixed_output(local_ref, entry_ref, conv_ref, cum_ref, gate_ref)
    ssd_ref[...] = ssd
    grad_norm = dot_low(cot_ref[...], w_out_ref[...], NT)
    grad_norm_ref[...] = grad_norm
    squares = jnp.sum(gated * gated, axis=-1, keepdims=True)
    inner_prod = jnp.sum(grad_norm * gain_ref[...] * gated, axis=-1, keepdims=True)
    sums_ref[...] = sums_of(squares, inner_prod)


def add_plain(base_ref, own_ref, *refs):
    *got, out_ref = refs
    total = own_ref[...]
    for ref in got:
        total = total + ref[...]
    out_ref[...] = base_ref[...] + total


def gate_back(grad_norm, rate, cross, ssd, gate, gain, conv, cum, state, outs):
    dy_ref, dz_ref, norm_ref, grow_ref, entry_ref = outs
    inner = ssd.shape[1]
    state_w = (conv.shape[1] - inner) // 2
    sig = sigmoid(gate)
    silu = gate * sig
    gated = ssd * silu
    unit = gated * rate
    norm_ref[...] = (unit * gain).astype(BF16)
    grow_ref[...] = jnp.broadcast_to(
        jnp.sum(grad_norm * unit, axis=0, keepdims=True), (EDGE, inner)
    )
    grad_gated = rate * (grad_norm * gain) - unit * (rate * rate * cross / ED)
    dy = grad_gated * silu
    dy_ref[...] = dy
    dz_ref[...] = (grad_gated * ssd * (sig * (1.0 + gate * (1.0 - sig)))).astype(BF16)
    conv_c = conv[:, inner + state_w :]
    c_ssd = conv_c * sigmoid(conv_c)
    grown = jnp.exp(spread(cum, inner))
    entry_ref[:state_w, :] = dot_mix(c_ssd, grown * dy, TN)
    entry_ref[state_w:, :] = state[state_w:, :]


def second_gate(
    sums_ref, grad_norm_ref, ssd_ref, gate_ref, gain_ref, conv_ref, cum_ref, state_ref, *outs
):
    rate, cross = rate_of(sums_ref[...])
    gate_back(
        grad_norm_ref[...], rate, cross, ssd_ref[...], gate_ref[...], gain_ref[...],
        conv_ref[...], cum_ref[...], state_ref[...], outs,
    )


def first_gate(
    parts, where_ref, own_ref, other_ref, after_ref, before_ref, sums_ref, w_out_ref, ssd_ref,
    gate_ref, gain_ref, conv_ref, cum_ref, state_ref, low_ref, *outs
):
    *outs, whole_ref = outs
    gather_rows(where_ref, whole_ref, own_ref, other_ref, parts)
    grad_low = whole_ref[...].astype(BF16)
    low_ref[...] = grad_low
    grad_norm = dot_low(grad_low, w_out_ref[...], NT)
    rate, _ = rate_of(sums_ref[...])
    branch = after_ref[...] - before_ref[...].astype(F32)
    cross = jnp.sum(grad_low.astype(F32) * branch, axis=-1, keepdims=True) / rate
    gate_back(
        grad_norm, rate, cross, ssd_ref[...], gate_ref[...], gain_ref[...], conv_ref[...],
        cum_ref[...], state_ref[...], outs,
    )


def out_project(parts, where_ref, norm_ref, w_out_ref, keep_ref, send_ref, whole_ref):
    whole_ref[...] = dot_low(norm_ref[...], w_out_ref[...])
    deal_rows(where_ref, whole_ref, keep_ref, send_ref, parts)


def scan_back(
    dy_ref, ssd_ref, conv_ref, pad_ref, dt_ref, cum_ref, entry_ref, state_ref, later_ref,
    taps_ref, heads_ref, mixed_ref, ddt_ref, small_ref, heads_out_ref, line_ref
):
    tokens, inner = dy_ref.shape
    state_w = entry_ref.shape[0] - EDGE
    dy = dy_ref[...]
    conv = conv_ref[...]
    sig = sigmoid(conv)
    act = conv * sig
    x_ssd = act[:, :inner]
    b_ssd = act[:, inner : inner + state_w]
    c_ssd = act[:, inner + state_w :]
    heads = heads_ref[...]
    log_rate = -jnp.exp(heads[1:2, :])
    skip = spread(heads[2:3, :], inner)
    dt_val = dt_ref[...]
    step = softplus(dt_val)
    cum = cum_ref[...]
    cum_rows = cum.T
    cum_chan = spread(cum, inner)
    step_chan = spread(step, inner)
    last = cum_chan[tokens - 1 : tokens, :]
    tail = jnp.exp(last - cum_chan)
    scaled = x_ssd * step_chan
    entry = entry_ref[:state_w, :]
    later = later_ref[:state_w, :]
    lower = ordered(tokens)
    cross = jnp.where(lower, dot_mix(c_ssd, b_ssd, NT), 0.0)
    grad_cross = jnp.zeros((tokens, tokens), F32)
    grad_scaled = []
    for head in range(inner // HEAD):
        span = slice(head * HEAD, (head + 1) * HEAD)
        gap = cum[:, head : head + 1] - cum_rows[head : head + 1, :]
        decay = jnp.exp(jnp.minimum(gap, 0.0))
        grad_scaled.append(dot_mix(cross * decay, dy[:, span], TN))
        grad_cross = grad_cross + decay * dot_mix(dy[:, span], scaled[:, span], NT)
    grad_cross = jnp.where(lower, grad_cross, 0.0)
    grad_scaled = jnp.concatenate(grad_scaled, axis=1) + tail * dot_mix(b_ssd, later)
    grad_c = dot_mix(grad_cross, b_ssd) + dot_mix(jnp.exp(cum_chan) * dy, entry, NT)
    grad_b = dot_mix(grad_cross, c_ssd, TN) + dot_mix(tail * scaled, later, NT)
    grad_x = step_chan * grad_scaled + skip * dy
    hot = one_hot(inner)
    dx_prod = x_ssd * grad_scaled
    dy_x = dy * x_ssd
    grad_cum = dot_sum(dy * ssd_ref[...] - skip * dy_x - step_chan * dx_prod, hot)
    final = jnp.exp(last) * entry + state_ref[:state_w, :]
    at_end = jnp.broadcast_to(jnp.sum(later * final, axis=0, keepdims=True), (EDGE, inner))
    behind = dot_sum(lower.astype(F32), grad_cum, TN) + dot_sum(at_end, hot)[:1, :]
    grad_step = behind * log_rate + dot_sum(dx_prod, hot)
    grad_dt = grad_step * sigmoid(dt_val)
    ddt_ref[...] = grad_dt.astype(BF16)
    skip_sum = jnp.broadcast_to(jnp.sum(dy_x, axis=0, keepdims=True), (EDGE, inner))
    row = lax.broadcasted_iota(jnp.int32, (EDGE, LANES), 0)
    heads_out_ref[...] = jnp.where(
        row == 0,
        jnp.sum(grad_dt, axis=0, keepdims=True),
        jnp.where(
            row == 1,
            jnp.sum(step * behind, axis=0, keepdims=True) * log_rate,
            jnp.where(row == 2, dot_sum(skip_sum, hot), 0.0),
        ),
    )
    grad_conv = jnp.concatenate([grad_x, grad_b, grad_c], axis=1) * (
        sig * (1.0 + conv * (1.0 - sig))
    )
    channels = conv.shape[1]
    line_ref[: 2 * EDGE, :] = jnp.zeros((2 * EDGE, channels), F32)
    line_ref[2 * EDGE : 2 * EDGE + tokens, :] = grad_conv
    line_ref[2 * EDGE + tokens :, :] = jnp.zeros((EDGE, channels), F32)
    mixed = jnp.zeros((tokens + EDGE, channels), F32)
    for tap in range(CONV):
        first = EDGE + CONV - 1 - tap
        mixed = mixed + taps_ref[tap : tap + 1, :] * line_ref[first : first + tokens + EDGE, :]
        first = EDGE - CONV + 1 + tap
        small_ref[tap : tap + 1, :] = jnp.sum(
            grad_conv * pad_ref[first : first + tokens, :], axis=0, keepdims=True
        )
    small_ref[CONV : CONV + 1, :] = jnp.sum(grad_conv, axis=0, keepdims=True)
    small_ref[CONV + 1 :, :] = jnp.zeros((EDGE - CONV - 1, channels), F32)
    mixed_ref[...] = mixed


def normed_back(
    parts, where_ref, mixed_ref, next_ref, dz_ref, ddt_ref, zx_ref, bc_ref, dt_ref, in_ref,
    x_low_ref, bc_ref_out, gain_ref, keep_ref, send_ref, whole_ref
):
    tokens = mixed_ref.shape[0] - EDGE
    inner = dz_ref.shape[1]
    fill = jnp.zeros((tokens - EDGE, mixed_ref.shape[1]), F32)
    mixed = mixed_ref[EDGE:, :] + jnp.concatenate([fill, next_ref[...]], axis=0)
    x_low = mixed[:, :inner].astype(BF16)
    x_low_ref[...] = x_low
    grad_bc = mixed[:, inner:]
    bc_ref_out[...] = grad_bc
    high, rest = halves(grad_bc)
    total = (
        dot_low(dz_ref[...], zx_ref[:, :inner], NT)
        + dot_low(x_low, zx_ref[:, inner:], NT)
        + dot_low(high, bc_ref[...], NT)
        + dot_low(rest, bc_ref[...], NT)
        + dot_low(ddt_ref[...], dt_ref[...], NT)
    )
    whole_ref[...] = total
    block_in = in_ref[...].astype(F32)
    scale = lax.rsqrt(jnp.mean(block_in * block_in, axis=-1, keepdims=True) + EPS)
    gain_ref[...] = jnp.broadcast_to(
        jnp.sum(total * block_in * scale, axis=0, keepdims=True), (EDGE, total.shape[1])
    )
    deal_rows(where_ref, whole_ref, keep_ref, send_ref, parts)


def input_back(grad_ref, in_ref, gain_ref, own_ref, *refs):
    *got, out_ref = refs
    total = own_ref[...]
    for ref in got:
        total = total + ref[...]
    block_in = in_ref[...]
    scale = lax.rsqrt(jnp.mean(block_in * block_in, axis=-1, keepdims=True) + EPS)
    weighted = total * gain_ref[...]
    inner_prod = jnp.mean(weighted * block_in, axis=-1, keepdims=True)
    out_ref[...] = (
        grad_ref[...] + scale * weighted - block_in * (scale * scale * scale * inner_prod)
    )


def lay_out(parts, where_ref, *refs):
    *pieces, out_ref = refs
    section = where_ref[0]
    micro = out_ref.shape[0]
    rows = pieces[0].shape[0] // parts
    for index in range(micro):
        lower = pieces[2 * index : 2 * index + 2]
        upper = pieces[2 * (micro + index) : 2 * (micro + index) + 2]
        for half in range(2):
            for part in range(parts):
                span = slice(part * rows, (part + 1) * rows)
                start = place(where_ref, half, part, parts, rows)
                out_ref[index, pl.ds(start, rows), :] = jnp.where(
                    section == 0, lower[half][span, :], upper[half][span, :]
                )


def swap(block):
    return lax.ppermute(block, "section", [(0, 1), (1, 0)])


def across(block, mask):
    count = lax.axis_size("head")
    return lax.ppermute(block, "head", [(i, i ^ mask) for i in range(count)])


def along(block, distance):
    devices = range(lax.axis_size("seq"))
    return lax.ppermute(
        block, "seq", [(i, i + distance) for i in devices if i + distance in devices]
    )


def carried(own, direction):
    depth = own.shape[0] - EDGE

    def combine(near, far):
        decay = near[depth : depth + 1]
        return jnp.concatenate(
            [near[:depth] + jnp.exp(decay) * far[:depth], near[depth:] + far[depth:]]
        )

    count = lax.axis_size("seq")
    covered = along(own, direction)
    distance = 2
    while distance < count:
        window = combine(own, covered)
        covered = combine(covered, along(window, direction * distance))
        distance *= 2
    return covered


def scatter_rows(keep, send):
    parts = lax.axis_size("head")
    both = keep + swap(send)
    rows = both.shape[0] // parts
    pieces = [both[part * rows : (part + 1) * rows] for part in range(parts)]
    return [pieces[0]] + [across(pieces[part], part) for part in range(1, parts)]


def collect_rows(piece):
    parts = lax.axis_size("head")
    own = jnp.concatenate([piece] + [across(piece, part) for part in range(1, parts)])
    return own, swap(own)


def on_device(
    inputs, cotangent, in_gain, w_z, w_x, w_bc, w_dt, dt_bias, a_log, skip, conv_x, conv_bc,
    convb_x, convb_bc, norm_gain, w_out
):
    section = lax.axis_index("section")
    head = lax.axis_index("head")
    parts = lax.axis_size("head")
    where = jnp.stack([section, head]).astype(jnp.int32)
    micro, tokens, model_w = inputs.shape
    inner = w_z.shape[2] // 2
    heads_n = w_dt.shape[2] // 2
    state_loc = w_bc.shape[3]
    state_w = state_loc * parts
    channels = inner + 2 * state_w
    rows = tokens // (2 * parts)
    mine = section == 0

    def other_half(whole, axis):
        size = whole.shape[axis] // 2
        return lax.dynamic_slice_in_dim(whole, (1 - section) * size, size, axis).astype(F32)

    def share(whole, axis):
        size = whole.shape[axis] // 2
        own = lax.dynamic_slice_in_dim(whole, section * size, size, axis)
        got = swap(other_half(whole, axis))
        return jnp.where(mine, own, got), jnp.where(mine, got, own)

    pack = jnp.concatenate([w_bc[0].astype(F32), conv_bc[0], convb_bc], axis=0)
    pack = pack.reshape(model_w + CONV + 1, 2 * state_loc)
    pack = jnp.concatenate([pack, jnp.zeros((EDGE - CONV - 1, 2 * state_loc), F32)], axis=0)
    gathered = [pack] + [across(pack, part) for part in range(1, parts)]
    narrow = jnp.pad(w_dt[0].astype(F32), ((0, EDGE), (0, LANES - 2 * heads_n)))
    own_pack = jnp.concatenate(
        [one[:, :state_loc] for one in gathered]
        + [one[:, state_loc:] for one in gathered]
        + [narrow],
        axis=1,
    )
    other_pack = swap(own_pack)
    got_zx = swap(jnp.concatenate([other_half(w_z[0], 1), other_half(w_x[0], 1)], axis=1))
    got_out = swap(other_half(w_out[0], 0))
    picked = kernel_call(
        functools.partial(pick_weights, heads_n=heads_n),
        [((model_w, 2 * inner), BF16)] * 2
        + [((model_w, 2 * state_w), BF16)] * 2
        + [((model_w, LANES), BF16)] * 2
        + [((inner, model_w), BF16)] * 2,
        (where, w_z[0], w_x[0], w_out[0], got_zx, got_out, own_pack, other_pack),
        4,
    )
    w_zxs, w_bcs, w_dts, w_outs = (picked[2 * at : 2 * at + 2] for at in range(4))
    own_rows = own_pack[model_w:, : 2 * state_w]
    other_rows = other_pack[model_w:, : 2 * state_w]
    pack_rows = (jnp.where(mine, own_rows, other_rows), jnp.where(mine, other_rows, own_rows))
    conv_xs = share(jnp.concatenate([conv_x[0], convb_x, norm_gain], axis=0), 1)
    head_rows = share(jnp.concatenate([dt_bias, a_log, skip], axis=0), 1)
    head_rows = [jnp.pad(one, ((0, EDGE - 3), (0, LANES - heads_n))) for one in head_rows]
    other_gain = swap(in_gain)
    in_gains = (jnp.where(mine, in_gain, other_gain), jnp.where(mine, other_gain, in_gain))
    taps = []
    gains = []
    for conv_part, pack_part in zip(conv_xs, pack_rows):
        five = jnp.concatenate([conv_part[: CONV + 1], pack_part[: CONV + 1]], axis=1)
        taps.append(jnp.pad(five, ((0, EDGE - CONV - 1), (0, 0))))
        gains.append(conv_part[CONV + 1 : CONV + 2])

    start = (section * parts + head) * rows
    chunk_in = lax.dynamic_slice_in_dim(inputs, start, rows, 1).astype(F32)
    chunk_cot = lax.dynamic_slice_in_dim(cotangent, start, rows, 1).astype(F32)
    halo_in = along(inputs[:, tokens - EDGE :].astype(F32), 1)

    project_outs = [
        ((tokens, model_w), BF16),
        ((tokens, inner), F32),
        ((tokens + EDGE, channels), F32),
        ((tokens, channels), F32),
        ((tokens, LANES), F32),
        ((tokens, LANES), F32),
        ((tokens, inner), F32),
        ((state_w + EDGE, inner), F32),
    ]
    half_rows = tokens // 2

    def summed(sums):
        sums = sums + swap(sums)
        got = [across(sums, part) for part in range(1, parts)]
        return functools.reduce(jnp.add, got, sums)

    def forward_first(index):
        normed, gate, pad, conv, dt_val, cum, local, state = kernel_call(
            first_forward, project_outs,
            (inputs[index], halo_in[index], in_gains[0], w_zxs[0], w_bcs[0], w_dts[0], taps[0],
             head_rows[0]),
            5, scalars=False,
        )
        entry = carried(state, 1)
        ssd, sums = kernel_call(
            first_output, [((tokens, inner), F32), ((EDGE, tokens), F32)],
            (local, entry, conv, cum, gate), 2, scalars=False,
        )
        sums = summed(sums)
        norm_out, keep, send = kernel_call(
            functools.partial(first_branch, parts),
            [((tokens, inner), BF16), ((half_rows, model_w), F32), ((half_rows, model_w), F32)],
            (where, sums, ssd, gate, gains[0], w_outs[0]),
            2, scratch=[pltpu.VMEM((tokens, model_w), F32)],
        )
        (chunk,) = kernel_call(
            add_plain, [((rows, model_w), F32)], (chunk_in[index], *scatter_rows(keep, send)), 1,
            scalars=False,
        )
        own, other = collect_rows(chunk)
        kept = (normed, gate, pad, conv, dt_val, cum, state, entry, ssd)
        return kept, chunk, own, other, sums

    def forward_second(index, own, other):
        top = jnp.where(mine, other, own)
        at = jnp.bitwise_xor(head, parts - 1) * rows + rows - EDGE
        halo = along(lax.dynamic_slice_in_dim(top, at, EDGE, 0), 1)
        block_in, normed, gate, pad, conv, dt_val, cum, local, state = kernel_call(
            functools.partial(later_forward, parts),
            [((tokens, model_w), F32)] + project_outs,
            (where, own, other, halo, in_gains[1], w_zxs[1], w_bcs[1], w_dts[1], taps[1],
             head_rows[1]),
            5,
        )
        entry = carried(state, 1)
        ssd, grad_norm, sums = kernel_call(
            second_output,
            [((tokens, inner), F32), ((tokens, inner), F32), ((EDGE, tokens), F32)],
            (local, entry, conv, cum, gate, gains[1], w_outs[1], cotangent[index]),
            3, scalars=False,
        )
        sums = summed(sums)
        kept = (normed, gate, pad, conv, dt_val, cum, state, entry, ssd)
        return kept, block_in, grad_norm, sums

    gate_outs = [
        ((tokens, inner), F32),
        ((tokens, inner), BF16),
        ((tokens, inner), BF16),
        ((EDGE, inner), F32),
        ((state_w + EDGE, inner), F32),
    ]

    def back_rest(block, kept, dy, dz, grad_entry, block_in):
        normed, gate, pad, conv, dt_val, cum, state, entry, ssd = kept
        later = carried(grad_entry, -1)
        mixed, ddt, small, head_sums = kernel_call(
            scan_back,
            [((tokens + EDGE, channels), F32), ((tokens, LANES), BF16), ((EDGE, channels), F32),
             ((EDGE, LANES), F32)],
            (dy, ssd, conv, pad, dt_val, cum, entry, state, later, taps[block], head_rows[block]),
            9, scratch=[pltpu.VMEM((tokens + 3 * EDGE, channels), F32)], scalars=False,
        )
        from_next = along(mixed[:EDGE], -1)
        x_low, grad_bc, gain_sum, keep, send = kernel_call(
            functools.partial(normed_back, parts),
            [((tokens, inner), BF16), ((tokens, 2 * state_w), F32), ((EDGE, model_w), F32),
             ((half_rows, model_w), F32), ((half_rows, model_w), F32)],
            (where, mixed, from_next, dz, ddt, w_zxs[block], w_bcs[block], w_dts[block], block_in),
            4, scratch=[pltpu.VMEM((tokens, model_w), F32)],
        )
        return x_low, ddt, grad_bc, small, head_sums, gain_sum, keep, send

    def input_grad(block, grad_chunk, in_chunk, keep, send):
        (chunk,) = kernel_call(
            input_back, [((rows, model_w), F32)],
            (grad_chunk, in_chunk, in_gains[block], *scatter_rows(keep, send)), 1, scalars=False,
        )
        return chunk

    def weight_grads(normed_all, dz_all, norm_all, grad_all, rest_all, grow_all):
        def over_tokens(lefts, rights):
            return functools.reduce(
                jnp.add, [dot_low(a, b, TN) for a, b in zip(lefts, rights)]
            )

        def total(values):
            return functools.reduce(jnp.add, values)

        x_low, ddt, grad_bc, small, head_sums, gain_sum = zip(*[one[:6] for one in rest_all])
        g_w_out = lax.psum_scatter(
            over_tokens(norm_all, grad_all), "seq", scatter_dimension=1, tiled=True
        )
        g_w_z = lax.psum_scatter(
            over_tokens(normed_all, dz_all), "seq", scatter_dimension=0, tiled=True
        )
        g_w_x = lax.psum_scatter(
            over_tokens(normed_all, x_low), "seq", scatter_dimension=0, tiled=True
        )
        kept_bc = jnp.where(mine, grad_bc[0], grad_bc[1])
        sent_bc = jnp.where(mine, grad_bc[1], grad_bc[0])
        small_bc = total([one[:, inner:] for one in small])
        own_bc = jnp.concatenate([kept_bc + swap(sent_bc), small_bc], axis=0)

        def part_of(part):
            low = part * state_loc
            return jnp.concatenate(
                [own_bc[:, low : low + state_loc],
                 own_bc[:, state_w + low : state_w + low + state_loc]], axis=1
            )

        sum_bc = functools.reduce(
            jnp.add, [across(part_of(part), part) for part in range(1, parts)], part_of(0)
        )
        bc_low = sum_bc[:tokens].astype(BF16)
        normed_own = jnp.where(mine, normed_all[0], normed_all[1])
        g_narrow = jnp.concatenate(
            [dot_low(normed_own, bc_low, TN), over_tokens(normed_all, ddt)[:, :heads_n]], axis=1
        )
        g_narrow = lax.psum_scatter(g_narrow, "seq", scatter_dimension=0, tiled=True)
        grow = total([one[:1] for one in grow_all])
        gain = total([one[:1] for one in gain_sum])
        row_set = lax.psum(
            (
                total([one[:, :inner] for one in small]),
                sum_bc[tokens:],
                grow,
                total(head_sums),
            ),
            "seq",
        )
        gain = lax.psum(gain, ("section", "seq", "head"))
        return g_w_z, g_w_x, g_w_out, g_narrow, row_set, gain

    firsts = [forward_first(index) for index in range(micro)]
    seconds = [forward_second(index, firsts[index][2], firsts[index][3]) for index in range(micro)]

    gates = []
    rests = []
    grads = []
    for index in range(micro):
        kept, block_in, grad_norm, sums = seconds[index]
        gates.append(
            kernel_call(
                second_gate, gate_outs,
                (sums, grad_norm, kept[8], kept[1], gains[1], kept[3], kept[5], kept[6]),
                4, scalars=False,
            )
        )
    for index in range(micro):
        kept, block_in = seconds[index][:2]
        dy, dz, norm_out, grow, grad_entry = gates[index]
        rest = back_rest(1, kept, dy, dz, grad_entry, block_in)
        rests.append(rest)
        grads.append(
            input_grad(1, chunk_cot[index], firsts[index][1], rest[6], rest[7])
        )
    upper = []
    for index in range(micro):
        keep, send = kernel_call(
            functools.partial(out_project, parts),
            [((half_rows, model_w), F32), ((half_rows, model_w), F32)],
            (where, gates[index][2], w_outs[1]),
            2, scratch=[pltpu.VMEM((tokens, model_w), F32)],
        )
        (chunk,) = kernel_call(
            add_plain, [((rows, model_w), F32)], (firsts[index][1], *scatter_rows(keep, send)), 1,
            scalars=False,
        )
        upper.extend(collect_rows(chunk))
    top_set = weight_grads(
        [one[0][0] for one in seconds], [one[1] for one in gates], [one[2] for one in gates],
        [cotangent[index] for index in range(micro)], rests, [one[3] for one in gates],
    )

    gates = []
    rests = []
    lows = []
    lower = []
    for index in range(micro):
        own, other = collect_rows(grads[index])
        kept = firsts[index][0]
        block_in = seconds[index][1]
        sums = firsts[index][4]
        low, *gate_set = kernel_call(
            functools.partial(first_gate, parts), [((tokens, model_w), BF16)] + gate_outs,
            (where, own, other, block_in, inputs[index], sums, w_outs[0], kept[8], kept[1],
             gains[0], kept[3], kept[5], kept[6]),
            5, scratch=[pltpu.VMEM((tokens, model_w), F32)],
        )
        lows.append(low)
        gates.append(gate_set)
    for index in range(micro):
        kept = firsts[index][0]
        dy, dz, norm_out, grow, grad_entry = gates[index]
        rest = back_rest(0, kept, dy, dz, grad_entry, inputs[index])
        rests.append(rest)
        chunk = input_grad(0, grads[index], chunk_in[index], rest[6], rest[7])
        lower.extend(collect_rows(chunk))
    low_set = weight_grads(
        [one[0][0] for one in firsts], [one[1] for one in gates], [one[2] for one in gates],
        lows, rests, [one[3] for one in gates],
    )

    (ends,) = kernel_call(
        functools.partial(lay_out, parts), [((micro, tokens, model_w), F32)],
        (where, *lower, *upper), 2,
    )

    def own_block(index):
        return jnp.where(mine, low_set[index], top_set[index])

    def whole_of(index, axis):
        own = own_block(index)
        got = swap(jnp.where(mine, top_set[index], low_set[index]))
        return jnp.concatenate(
            [jnp.where(mine, own, got), jnp.where(mine, got, own)], axis=axis
        )

    g_w_z = whole_of(0, 1)
    g_w_x = whole_of(1, 1)
    g_w_out = whole_of(2, 0)
    own_narrow = own_block(3)
    got_narrow = swap(jnp.where(mine, top_set[3], low_set[3]))
    g_w_bc = (own_narrow + got_narrow)[:, : 2 * state_loc].reshape(-1, 2, state_loc)
    own_dt = own_narrow[:, 2 * state_loc :]
    got_dt = got_narrow[:, 2 * state_loc :]
    g_w_dt = jnp.concatenate(
        [jnp.where(mine, own_dt, got_dt), jnp.where(mine, got_dt, own_dt)], axis=1
    )
    low_rows, top_rows = low_set[4], top_set[4]
    bc_rows = [jnp.where(mine, low_rows[1], top_rows[1]), jnp.where(mine, top_rows[1], low_rows[1])]
    bc_rows = bc_rows[0] + swap(bc_rows[1])

    def widened(low_one, top_one):
        own = jnp.where(mine, low_one, top_one)
        got = swap(jnp.where(mine, top_one, low_one))
        return jnp.concatenate([jnp.where(mine, own, got), jnp.where(mine, got, own)], axis=1)

    x_rows = widened(low_rows[0], top_rows[0])
    g_norm_gain = widened(low_rows[2], top_rows[2])
    head_set = widened(low_rows[3][:, :heads_n], top_rows[3][:, :heads_n])
    g_in_gain = jnp.where(mine, low_set[5], top_set[5])
    return (
        ends[None],
        g_in_gain,
        g_w_z[None],
        g_w_x[None],
        g_w_bc[None],
        g_w_dt[None],
        head_set[0:1],
        head_set[1:2],
        head_set[2:3],
        x_rows[None, :CONV],
        bc_rows[:CONV].reshape(1, CONV, 2, state_loc),
        x_rows[CONV : CONV + 1],
        bc_rows[CONV : CONV + 1].reshape(1, 2, state_loc),
        g_norm_gain,
        g_w_out[None],
    )


def solution(mesh):
    in_specs = (
        P(None, "seq", None),
        P(None, "seq", None),
        P("section", None),
        P("section", None, "head"),
        P("section", None, "head"),
        P("section", None, None, "head"),
        P("section", None, "head"),
        P("section", "head"),
        P("section", "head"),
        P("section", "head"),
        P("section", None, "head"),
        P("section", None, None, "head"),
        P("section", "head"),
        P("section", None, "head"),
        P("section", "head"),
        P("section", "head", None),
    )
    out_specs = (
        P("section", None, "seq", None),
        P("section", None),
        P("section", "seq", "head"),
        P("section", "seq", "head"),
        P("section", "seq", None, "head"),
        P("section", "seq", "head"),
        P("section", "head"),
        P("section", "head"),
        P("section", "head"),
        P("section", None, "head"),
        P("section", None, None, "head"),
        P("section", "head"),
        P("section", None, "head"),
        P("section", "head"),
        P("section", "head", "seq"),
    )
    return jax.shard_map(
        on_device, mesh=mesh, in_specs=in_specs, out_specs=out_specs, check_vma=False
    )
```

```python
import functools

import jax
import jax.numpy as jnp
from jax import lax
from jax.experimental import pallas as pl
from jax.experimental.pallas import tpu as pltpu
from jax.sharding import PartitionSpec as P

ED = 2048
HEAD = 64
CONV = 4
EPS = 1e-05
EDGE = 8
LANES = 128
VMEM_LIMIT = 20 * 1024 * 1024
F32 = jnp.float32
BF16 = jnp.bfloat16
NN = (((1,), (0,)), ((), ()))
NT = (((1,), (1,)), ((), ()))
TN = (((0,), (0,)), ((), ()))


SCHEDULE = (
    ("a", "b", "u0", "u1"),
    ("a", "u0", "b", "u1"),
    ("a", "u0", "b", "u1", "early1"),
    ("a", "u0", "b", "u1"),
    ("a", "b", "wide1", "narrow1"),
    ("a", "b", "early1", "narrow1"),
    ("a", "b", "narrow1", "narrow1"),
    ("a", "b", "early0"),
    ("a", "b", "wide1", "narrow1", "rows1"),
    ("a", "wide1", "narrow1", "b"),
    ("a", "b", "wide0", "narrow0"),
    ("a", "b", "narrow0", "early0", "rows1"),
    ("a", "b", "narrow0", "wide0", "narrow0"),
    ("tends", "early0", "tearly"),
    ("narrow0", "rows0", "wide0", "twide"),
    ("rows0", "narrow0", "tnarrow", "rows0", "trows"),
)


def dot_low(left, right, dims=NN):
    return lax.dot_general(left.astype(BF16), right.astype(BF16), dims, preferred_element_type=F32)


def halves(value):
    high = value.astype(BF16)
    return high, (value - high.astype(F32)).astype(BF16)


def dot_split(left, right, dims=NN):
    left_hi, left_lo = halves(left)
    right_hi, right_lo = halves(right)
    mul = functools.partial(lax.dot_general, dimension_numbers=dims, preferred_element_type=F32)
    return mul(left_hi, right_hi) + (mul(left_hi, right_lo) + mul(left_lo, right_hi))


def dot_exact(left, right, dims=NN):
    return lax.dot_general(
        left, right, dims, precision=lax.Precision.HIGHEST, preferred_element_type=F32
    )


dot_mix = dot_split
dot_sum = dot_exact


class Line:
    mark = None


class Kept:
    def __init__(self, value, index=None):
        self.value = value
        self.index = index


def kernel_call(body, outs, args, time_us, scratch=(), scalars=True, held=False):
    whole = pl.BlockSpec(memory_space=pltpu.VMEM)
    specs = []
    values = []
    for at, arg in enumerate(args):
        if scalars and at == 0:
            specs.append(pl.BlockSpec(memory_space=pltpu.SMEM))
            values.append(arg)
        elif isinstance(arg, Kept):
            value = arg.value
            if held:
                value = pltpu.with_memory_space_constraint(value, pltpu.HBM)
            values.append(value)
            specs.append(whole)
        else:
            values.append(pltpu.with_memory_space_constraint(arg, pltpu.VMEM))
            specs.append(whole)
    places = [arg.index if isinstance(arg, Kept) else None for arg in args]
    before = [] if Line.mark is None else [Line.mark]
    specs.extend([pl.BlockSpec(memory_space=pl.ANY)] * len(before))
    inputs_n = len(args) + len(before)

    def viewed(*refs):
        views = [
            ref if at is None else ref.at[at] for ref, at in zip(refs, places)
        ]
        refs[inputs_n][...] = jnp.zeros((EDGE, LANES), F32)
        body(*views, *refs[inputs_n + 1 :])

    results = pl.pallas_call(
        viewed,
        out_shape=[pltpu.VMEM((EDGE, LANES), F32)]
        + [(pltpu.HBM if len(out) > 2 else pltpu.VMEM)(out[0], out[1]) for out in outs],
        in_specs=specs,
        out_specs=[whole] * (1 + len(outs)),
        scratch_shapes=list(scratch),
        compiler_params=pltpu.CompilerParams(vmem_limit_bytes=VMEM_LIMIT),
        cost_estimate=pl.CostEstimate(
            flops=0, bytes_accessed=int(time_us * 3_000_000), transcendentals=0
        ),
    )(*values, *before)
    Line.mark, *results = results
    return [
        Kept(result) if len(out) > 2 else result for out, result in zip(outs, results)
    ]


def sigmoid(values):
    return 1.0 / (1.0 + jnp.exp(-values))


def softplus(values):
    return jnp.maximum(values, 0.0) + jnp.log1p(jnp.exp(-jnp.abs(values)))


def one_hot(channels):
    head_of = lax.broadcasted_iota(jnp.int32, (channels, LANES), 0) // HEAD
    return (head_of == lax.broadcasted_iota(jnp.int32, (channels, LANES), 1)).astype(F32)


def spread(per_head, channels):
    rows = per_head.shape[0]
    return jnp.concatenate(
        [
            jnp.broadcast_to(per_head[:, head : head + 1], (rows, HEAD))
            for head in range(channels // HEAD)
        ],
        axis=1,
    )


def ordered(tokens):
    row = lax.broadcasted_iota(jnp.int32, (tokens, tokens), 0)
    col = lax.broadcasted_iota(jnp.int32, (tokens, tokens), 1)
    return row >= col


def half_at(where_ref, side, rows):
    start = (where_ref[0] if side == 0 else 1 - where_ref[0]) * rows
    return pl.ds(pl.multiple_of(start, rows), rows)


def gather_rows(where_ref, target_ref, own_ref, other_ref):
    rows = own_ref.shape[0]
    target_ref[half_at(where_ref, 0, rows), :] = own_ref[...]
    target_ref[half_at(where_ref, 1, rows), :] = other_ref[...]


def deal_rows(where_ref, source_ref, keep_ref, send_ref):
    rows = keep_ref.shape[0]
    keep_ref[...] = source_ref[half_at(where_ref, 0, rows), :]
    send_ref[...] = source_ref[half_at(where_ref, 1, rows), :]


def deal_chunks(where_ref, rows, step, read, keep_ref, send_ref):
    bit = jnp.bitwise_and(lax.shift_right_logical(where_ref[1], step), 1)
    for at in range(keep_ref.shape[0] // rows):
        span = slice(at * rows, (at + 1) * rows)
        start = pl.multiple_of((2 * at + bit) * rows, rows)
        keep_ref[span, :] = read(pl.ds(start, rows))
        start = pl.multiple_of((2 * at + 1 - bit) * rows, rows)
        send_ref[span, :] = read(pl.ds(start, rows))


def add_chunks(where_ref, left_ref, right_ref, keep_ref, send_ref, *, rows, step):
    deal_chunks(
        where_ref, rows, step, lambda span: left_ref[span, :] + right_ref[span, :], keep_ref,
        send_ref,
    )


def add_pair(left_ref, right_ref, out_ref):
    out_ref[...] = left_ref[...] + right_ref[...]


def pick_pair(where_ref, first_ref, second_ref, own_ref, other_ref):
    @pl.when(where_ref[0] == 0)
    def _():
        own_ref[...] = first_ref[...]
        other_ref[...] = second_ref[...]

    @pl.when(where_ref[0] != 0)
    def _():
        own_ref[...] = second_ref[...]
        other_ref[...] = first_ref[...]


def pick_sums(where_ref, low_ref, low_got_ref, top_ref, top_got_ref, own_ref, other_ref):
    low = low_ref[...] + low_got_ref[...]
    top = top_ref[...] + top_got_ref[...]
    own_ref[...] = jnp.where(where_ref[0] == 0, low, top)
    other_ref[...] = jnp.where(where_ref[0] == 0, top, low)


def join_sides(where_ref, own, got, axis):
    first = jnp.where(where_ref[0] == 0, own, got)
    second = jnp.where(where_ref[0] == 0, got, own)
    return jnp.concatenate([first, second], axis=axis)


def join_first(where_ref, own_ref, got_ref, z_ref, out_ref):
    width = own_ref.shape[1] // 2
    z_ref[...] = join_sides(where_ref, own_ref[:, :width], got_ref[:, :width], 1)
    out_ref[...] = join_sides(where_ref, own_ref[:, width:].T, got_ref[:, width:].T, 0)


def join_second(where_ref, own_ref, got_ref, x_ref):
    x_ref[...] = join_sides(where_ref, own_ref[...], got_ref[...], 1)


def join_rows(
    where_ref, own_ref, got_ref, conv_ref, convb_ref, norm_ref, gain_ref, bias_ref, log_ref,
    skip_ref, bc_ref
):
    own = own_ref[...]
    got = got_ref[...]
    inner = conv_ref.shape[1] // 2
    heads_n = bias_ref.shape[1] // 2
    both = join_sides(where_ref, own[:EDGE, :inner], got[:EDGE, :inner], 1)
    conv_ref[...] = both[:CONV]
    convb_ref[...] = both[CONV : CONV + 1]
    norm_ref[...] = both[CONV + 1 : CONV + 2]
    total = own + got
    gain_ref[...] = total[CONV + 2 : CONV + 3]
    heads = join_sides(where_ref, own[EDGE:, :heads_n], got[EDGE:, :heads_n], 1)
    bias_ref[...] = heads[0:1]
    log_ref[...] = heads[1:2]
    skip_ref[...] = heads[2:3]
    bc_ref[...] = total[EDGE:, LANES : LANES + bc_ref.shape[1]]


def join_window(own_ref, near_ref, window_ref):
    depth = own_ref.shape[0] - EDGE
    decay = own_ref[depth : depth + 1, :]
    window_ref[:depth, :] = own_ref[:depth, :] + jnp.exp(decay) * near_ref[:depth, :]
    window_ref[depth:, :] = own_ref[depth:, :] + near_ref[depth:, :]


def pack_weights(
    where_ref, in_ref, z_ref, x_ref, out_ref, bc_ref, conv_bc_ref, convb_bc_ref, dt_ref, conv_x_ref,
    convb_x_ref, gain_ref, in_gain_ref, bias_ref, log_ref, skip_ref,
    pack_ref, send_zx_ref, send_out_ref, rows_ref, edge_ref
):
    edge_ref[...] = in_ref[:, in_ref.shape[1] - EDGE :, :].astype(F32)
    model_w, width = z_ref.shape
    inner = width // 2
    half = model_w // 2
    pair = bc_ref.shape[1]
    there = half_at(where_ref, 1, inner)
    pack_ref[:half, :pair] = bc_ref[:half, :].astype(F32)
    pack_ref[:half, pair:] = bc_ref[half:, :].astype(F32)
    pack_ref[half:, :] = jnp.zeros((EDGE, 2 * pair), F32)
    pack_ref[half : half + CONV, :pair] = conv_bc_ref[...]
    pack_ref[half + CONV : half + CONV + 1, :pair] = convb_bc_ref[...]
    send_zx_ref[:, :inner] = z_ref[:, there].astype(F32)
    send_zx_ref[:, inner:] = x_ref[:, there].astype(F32)
    send_out_ref[...] = out_ref[there, :].astype(F32)
    heads_n = dt_ref.shape[1]
    rows_ref[...] = jnp.zeros(rows_ref.shape, F32)
    rows_ref[:CONV, :width] = conv_x_ref[...]
    rows_ref[CONV : CONV + 1, :width] = convb_x_ref[...]
    rows_ref[CONV + 1 : CONV + 2, :width] = gain_ref[...]
    rows_ref[CONV + 2 : CONV + 3, :] = in_gain_ref[...]
    rows_ref[EDGE : EDGE + 1, :heads_n] = bias_ref[...]
    rows_ref[EDGE + 1 : EDGE + 2, :heads_n] = log_ref[...]
    rows_ref[EDGE + 2 : EDGE + 3, :heads_n] = skip_ref[...]
    rows_ref[2 * EDGE : 2 * EDGE + heads_n, :] = dt_ref[...].astype(F32).T


def pick_weights(
    where_ref, z_ref, x_ref, out_ref, got_zx_ref, got_out_ref, own_rows_ref, got_rows_ref,
    *refs, parts
):
    own_packs, got_packs, outs = refs[:parts], refs[parts : 2 * parts], refs[2 * parts :]
    section = where_ref[0]
    model_w = z_ref.shape[0]
    half = model_w // 2
    inner = got_zx_ref.shape[1] // 2
    pair = own_packs[0].shape[1] // 2
    heads_n = inner // HEAD
    here = half_at(where_ref, 0, inner)

    def side(value):
        return jnp.where(section == 0, value[:, :inner], value[:, inner : 2 * inner])

    def write(refs, zx, out_part, packs, rows_ref):
        zx_to, bc_to, dt_to, out_to, taps_to, heads_to, gain_to, in_to = refs
        zx_to[:, :inner] = zx[0]
        zx_to[:, inner:] = zx[1]
        out_to[...] = out_part
        loc = pair // 2
        order = [0, 2, 1, 3] if parts == 4 else list(range(parts))
        values = [packs[part][...] for part in order]

        def columns(low, top):
            return jnp.concatenate(
                [one[low:top, :loc] for one in values]
                + [one[low:top, loc:pair] for one in values],
                axis=1,
            )

        bc_to[:half, :] = columns(0, half).astype(BF16)
        bc_to[half:, :] = jnp.concatenate(
            [one[:half, pair : pair + loc] for one in values]
            + [one[:half, pair + loc :] for one in values],
            axis=1,
        ).astype(BF16)
        rows = rows_ref[...]
        taps_to[:, :inner] = side(rows[:EDGE])
        taps_to[:, inner:] = columns(half, half + EDGE)
        gain_to[...] = side(rows[CONV + 1 : CONV + 2])
        in_to[...] = rows[CONV + 2 : CONV + 3]
        lane = lax.broadcasted_iota(jnp.int32, (EDGE, LANES), 1)
        vecs = rows[EDGE : 2 * EDGE, :LANES]
        vecs = jnp.where(section == 0, vecs, pltpu.roll(vecs, LANES - heads_n, 1))
        heads_to[...] = jnp.where(lane < heads_n, vecs, 0.0)
        dt_rows = rows[2 * EDGE :]
        dt_rows = jnp.where(
            section == 0,
            dt_rows[:heads_n],
            dt_rows[heads_n : 2 * heads_n],
        )
        fill = jnp.zeros((LANES - heads_n, model_w), F32)
        dt_to[...] = jnp.concatenate([dt_rows, fill], axis=0).T.astype(BF16)

    own = ((z_ref[:, here], x_ref[:, here]), out_ref[here, :], own_packs, own_rows_ref)
    got = (
        (got_zx_ref[:, :inner].astype(BF16), got_zx_ref[:, inner:].astype(BF16)),
        got_out_ref[...].astype(BF16), got_packs, got_rows_ref,
    )
    first, second, now = outs[:8], outs[8:16], outs[16:]

    @pl.when(section == 0)
    def _():
        write(first, *own)
        write(now, *own)
        write(second, *got)

    @pl.when(section != 0)
    def _():
        write(first, *got)
        write(now, *got)
        write(second, *own)


def project(block_in, halo, in_gain, w_zx, w_bc, w_dt, taps, heads, outs):
    normed_ref, gate_ref, pad_ref, conv_ref, dt_ref, cum_ref, state_ref, *soon = outs
    gate_now_ref, c_now_ref, grown_ref, local_ref, state_now_ref = soon
    tokens = block_in.shape[0]
    inner = w_zx.shape[1] // 2
    rows = jnp.concatenate([halo, block_in], axis=0)
    scale = lax.rsqrt(jnp.mean(rows * rows, axis=-1, keepdims=True) + EPS)
    normed = (rows * scale * in_gain).astype(BF16)
    low = normed[EDGE:]
    normed_ref[...] = low
    gate = dot_low(low, w_zx[:, :inner])
    gate_ref[...] = gate
    gate_now_ref[...] = gate * sigmoid(gate)
    pad_ref[:, :inner] = dot_low(normed, w_zx[:, inner:])
    pad_ref[:, inner:] = dot_low(normed, w_bc)
    dt_val = dot_low(low, w_dt) + heads[0:1, :]
    dt_ref[...] = dt_val
    conv = taps[CONV : CONV + 1, :]
    for tap in range(CONV):
        first = EDGE - CONV + 1 + tap
        conv = conv + taps[tap : tap + 1, :] * pad_ref[first : first + tokens, :]
    conv_ref[...] = conv
    act = conv * sigmoid(conv)
    state_w = (act.shape[1] - inner) // 2
    x_ssd = act[:, :inner]
    b_ssd = act[:, inner : inner + state_w]
    c_ssd = act[:, inner + state_w :]
    c_now_ref[...] = c_ssd
    log_rate = -jnp.exp(heads[1:2, :])
    step = softplus(dt_val)
    lower = ordered(tokens)
    cum = dot_sum(lower.astype(F32), step * log_rate)
    cum_ref[...] = cum
    cum_rows = cum.T
    scaled = x_ssd * spread(step, inner)
    cross = jnp.where(lower, dot_mix(c_ssd, b_ssd, NT), 0.0)
    outputs = []
    for head in range(inner // HEAD):
        gap = cum[:, head : head + 1] - cum_rows[head : head + 1, :]
        mix = cross * jnp.exp(jnp.minimum(gap, 0.0))
        outputs.append(dot_mix(mix, scaled[:, head * HEAD : (head + 1) * HEAD]))
    local_ref[...] = jnp.concatenate(outputs, axis=1) + spread(heads[2:3, :], inner) * x_ssd
    cum_chan = spread(cum, inner)
    last = cum_chan[tokens - 1 : tokens, :]
    grown_ref[...] = jnp.exp(cum_chan)
    state_now_ref[:state_w, :] = dot_mix(b_ssd, scaled * jnp.exp(last - cum_chan), TN)
    state_now_ref[state_w:, :] = jnp.broadcast_to(last, (EDGE, inner))
    state_ref[...] = state_now_ref[...]


def first_forward(in_ref, halo_ref, gain_ref, zx_ref, bc_ref, dt_ref, taps_ref, heads_ref, *outs):
    project(
        in_ref[...].astype(F32), halo_ref[...], gain_ref[...], zx_ref[...], bc_ref[...],
        dt_ref[...], taps_ref[...], heads_ref[...], outs,
    )


def later_forward(
    where_ref, own_ref, other_ref, halo_ref, gain_ref, zx_ref, bc_ref, dt_ref, taps_ref,
    heads_ref, in_ref, *outs
):
    gather_rows(where_ref, in_ref, own_ref, other_ref)
    project(
        in_ref[...], halo_ref[...], gain_ref[...], zx_ref[...], bc_ref[...], dt_ref[...],
        taps_ref[...], heads_ref[...], outs,
    )


def entered(near, far):
    depth = near.shape[0] - EDGE
    return near[:depth] + jnp.exp(near[depth : depth + 1]) * far[:depth]


def mixed_output(local_ref, near_ref, far_ref, c_ref, grown_ref, gate_ref, entry_ref):
    entry = entered(near_ref[...], far_ref[...])
    entry_ref[...] = entry
    ssd = local_ref[...] + grown_ref[...] * dot_mix(c_ref[...], entry)
    return ssd, ssd * gate_ref[...]


def sums_of(squares, inner_prod):
    lane = lax.broadcasted_iota(jnp.int32, (squares.shape[0], LANES), 1)
    both = jnp.where(lane == 0, squares, jnp.where(lane == 1, inner_prod, 0.0))
    return both.T[:EDGE, :]


def rate_of(sums):
    fill = jnp.zeros((LANES - sums.shape[0], sums.shape[1]), F32)
    columns = jnp.concatenate([sums, fill], axis=0).T
    return lax.rsqrt(columns[:, :1] / ED + EPS), columns[:, 1:2]


def first_output(
    local_ref, near_ref, far_ref, c_ref, grown_ref, gate_ref,
    ssd_ref, entry_ref, gated_ref, sums_ref
):
    ssd, gated = mixed_output(
        local_ref, near_ref, far_ref, c_ref, grown_ref, gate_ref, entry_ref
    )
    ssd_ref[...] = ssd
    gated_ref[...] = gated
    sums_ref[...] = sums_of(jnp.sum(gated * gated, axis=-1, keepdims=True), 0.0)


def first_branch(
    where_ref, sums_ref, more_ref, gated_ref, gain_ref, w_out_ref, norm_ref, keep_ref, send_ref,
    sums_out_ref, whole_ref
):
    sums = sums_ref[...] + more_ref[...]
    rate, _ = rate_of(sums)
    sums_out_ref[...] = sums
    norm_out = (gated_ref[...] * rate * gain_ref[...]).astype(BF16)
    norm_ref[...] = norm_out
    whole_ref[...] = dot_low(norm_out, w_out_ref[...])
    deal_rows(where_ref, whole_ref, keep_ref, send_ref)


def second_output(
    local_ref, near_ref, far_ref, c_ref, grown_ref, gate_ref, gain_ref, w_out_ref, cot_ref,
    ssd_ref, entry_ref, grad_norm_ref, sums_ref
):
    ssd, gated = mixed_output(
        local_ref, near_ref, far_ref, c_ref, grown_ref, gate_ref, entry_ref
    )
    ssd_ref[...] = ssd
    grad_norm = dot_low(cot_ref[...], w_out_ref[...], NT)
    grad_norm_ref[...] = grad_norm
    squares = jnp.sum(gated * gated, axis=-1, keepdims=True)
    inner_prod = jnp.sum(grad_norm * gain_ref[...] * gated, axis=-1, keepdims=True)
    sums_ref[...] = sums_of(squares, inner_prod)


def add_split(left_ref, right_ref, first_ref, second_ref):
    rows = first_ref.shape[0]
    first_ref[...] = left_ref[:rows, :] + right_ref[:rows, :]
    second_ref[...] = left_ref[rows:, :] + right_ref[rows:, :]


def stacked(own_first, got_first, own_second, got_second):
    return jnp.concatenate(
        [own_first[...] + got_first[...], own_second[...] + got_second[...]], axis=0
    )


def add_base(where_ref, base_ref, *refs):
    *terms, out_ref, kept_ref = refs
    rows = out_ref.shape[0]
    base = base_ref[half_at(where_ref, 0, rows), :] if base_ref.shape[0] > rows else base_ref[...]
    total = base.astype(F32) + stacked(*terms)
    out_ref[...] = total
    kept_ref[...] = total


def gate_back(grad_norm, rate, cross, ssd, gate, gain, conv, cum, state, outs):
    dy_ref, dz_ref, norm_ref, grow_ref, entry_ref = outs
    inner = ssd.shape[1]
    state_w = (conv.shape[1] - inner) // 2
    sig = sigmoid(gate)
    silu = gate * sig
    gated = ssd * silu
    unit = gated * rate
    norm_ref[...] = (unit * gain).astype(BF16)
    grow_ref[...] = jnp.broadcast_to(
        jnp.sum(grad_norm * unit, axis=0, keepdims=True), (EDGE, inner)
    )
    grad_gated = rate * (grad_norm * gain) - unit * (rate * rate * cross / ED)
    dy = grad_gated * silu
    dy_ref[...] = dy
    dz_ref[...] = (grad_gated * ssd * (sig * (1.0 + gate * (1.0 - sig)))).astype(BF16)
    conv_c = conv[:, inner + state_w :]
    c_ssd = conv_c * sigmoid(conv_c)
    grown = jnp.exp(spread(cum, inner))
    entry_ref[:state_w, :] = dot_mix(c_ssd, grown * dy, TN)
    entry_ref[state_w:, :] = state[state_w:, :]


def second_gate(
    sums_ref, more_ref, grad_norm_ref, ssd_ref, gate_ref, gain_ref, conv_ref, cum_ref, state_ref, *outs
):
    rate, cross = rate_of(sums_ref[...] + more_ref[...])
    gate_back(
        grad_norm_ref[...], rate, cross, ssd_ref[...], gate_ref[...], gain_ref[...],
        conv_ref[...], cum_ref[...], state_ref[...], outs,
    )


def first_gate(
    where_ref, own_ref, other_ref, after_ref, before_ref, sums_ref, w_out_ref, ssd_ref,
    gate_ref, gain_ref, conv_ref, cum_ref, state_ref, low_ref, *outs
):
    *outs, whole_ref = outs
    gather_rows(where_ref, whole_ref, own_ref, other_ref)
    grad_low = whole_ref[...].astype(BF16)
    low_ref[...] = grad_low
    grad_norm = dot_low(grad_low, w_out_ref[...], NT)
    rate, _ = rate_of(sums_ref[...])
    branch = after_ref[...] - before_ref[...].astype(F32)
    cross = jnp.sum(grad_low.astype(F32) * branch, axis=-1, keepdims=True) / rate
    gate_back(
        grad_norm, rate, cross, ssd_ref[...], gate_ref[...], gain_ref[...], conv_ref[...],
        cum_ref[...], state_ref[...], outs,
    )


def out_project(where_ref, norm_ref, w_out_ref, keep_ref, send_ref, whole_ref):
    whole_ref[...] = dot_low(norm_ref[...], w_out_ref[...])
    deal_rows(where_ref, whole_ref, keep_ref, send_ref)


def scan_back(
    dy_ref, ssd_ref, conv_ref, pad_ref, dt_ref, cum_ref, entry_ref, state_ref, near_ref, far_ref,
    taps_ref, heads_ref, mixed_ref, ddt_ref, small_ref, heads_out_ref, line_ref
):
    tokens, inner = dy_ref.shape
    state_w = entry_ref.shape[0]
    dy = dy_ref[...]
    conv = conv_ref[...]
    sig = sigmoid(conv)
    act = conv * sig
    x_ssd = act[:, :inner]
    b_ssd = act[:, inner : inner + state_w]
    c_ssd = act[:, inner + state_w :]
    heads = heads_ref[...]
    log_rate = -jnp.exp(heads[1:2, :])
    skip = spread(heads[2:3, :], inner)
    dt_val = dt_ref[...]
    step = softplus(dt_val)
    cum = cum_ref[...]
    cum_rows = cum.T
    cum_chan = spread(cum, inner)
    step_chan = spread(step, inner)
    last = cum_chan[tokens - 1 : tokens, :]
    tail = jnp.exp(last - cum_chan)
    scaled = x_ssd * step_chan
    entry = entry_ref[...]
    later = entered(near_ref[...], far_ref[...])
    lower = ordered(tokens)
    cross = jnp.where(lower, dot_mix(c_ssd, b_ssd, NT), 0.0)
    grad_cross = jnp.zeros((tokens, tokens), F32)
    grad_scaled = []
    for head in range(inner // HEAD):
        span = slice(head * HEAD, (head + 1) * HEAD)
        gap = cum[:, head : head + 1] - cum_rows[head : head + 1, :]
        decay = jnp.exp(jnp.minimum(gap, 0.0))
        grad_scaled.append(dot_mix(cross * decay, dy[:, span], TN))
        grad_cross = grad_cross + decay * dot_mix(dy[:, span], scaled[:, span], NT)
    grad_cross = jnp.where(lower, grad_cross, 0.0)
    grad_scaled = jnp.concatenate(grad_scaled, axis=1) + tail * dot_mix(b_ssd, later)
    grad_c = dot_mix(grad_cross, b_ssd) + dot_mix(jnp.exp(cum_chan) * dy, entry, NT)
    grad_b = dot_mix(grad_cross, c_ssd, TN) + dot_mix(tail * scaled, later, NT)
    grad_x = step_chan * grad_scaled + skip * dy
    hot = one_hot(inner)
    dx_prod = x_ssd * grad_scaled
    dy_x = dy * x_ssd
    grad_cum = dot_sum(dy * ssd_ref[...] - skip * dy_x - step_chan * dx_prod, hot)
    final = jnp.exp(last) * entry + state_ref[:state_w, :]
    at_end = jnp.broadcast_to(jnp.sum(later * final, axis=0, keepdims=True), (EDGE, inner))
    behind = dot_sum(lower.astype(F32), grad_cum, TN) + dot_sum(at_end, hot)[:1, :]
    grad_step = behind * log_rate + dot_sum(dx_prod, hot)
    grad_dt = grad_step * sigmoid(dt_val)
    ddt_ref[...] = grad_dt.astype(BF16)
    skip_sum = jnp.broadcast_to(jnp.sum(dy_x, axis=0, keepdims=True), (EDGE, inner))
    row = lax.broadcasted_iota(jnp.int32, (EDGE, LANES), 0)
    heads_out_ref[...] = jnp.where(
        row == 0,
        jnp.sum(grad_dt, axis=0, keepdims=True),
        jnp.where(
            row == 1,
            jnp.sum(step * behind, axis=0, keepdims=True) * log_rate,
            jnp.where(row == 2, dot_sum(skip_sum, hot), 0.0),
        ),
    )
    grad_conv = jnp.concatenate([grad_x, grad_b, grad_c], axis=1) * (
        sig * (1.0 + conv * (1.0 - sig))
    )
    channels = conv.shape[1]
    line_ref[: 2 * EDGE, :] = jnp.zeros((2 * EDGE, channels), F32)
    line_ref[2 * EDGE : 2 * EDGE + tokens, :] = grad_conv
    line_ref[2 * EDGE + tokens :, :] = jnp.zeros((EDGE, channels), F32)
    mixed = jnp.zeros((tokens + EDGE, channels), F32)
    for tap in range(CONV):
        first = EDGE + CONV - 1 - tap
        mixed = mixed + taps_ref[tap : tap + 1, :] * line_ref[first : first + tokens + EDGE, :]
        first = EDGE - CONV + 1 + tap
        small_ref[tap : tap + 1, :] = jnp.sum(
            grad_conv * pad_ref[first : first + tokens, :], axis=0, keepdims=True
        )
    small_ref[CONV : CONV + 1, :] = jnp.sum(grad_conv, axis=0, keepdims=True)
    small_ref[CONV + 1 :, :] = jnp.zeros((EDGE - CONV - 1, channels), F32)
    mixed_ref[...] = mixed


def normed_back(
    where_ref, mixed_ref, next_ref, small_ref, dz_ref, ddt_ref, zx_ref, bc_ref, dt_ref,
    x_low_ref, bc_out_ref, keep_ref, send_ref, whole_ref
):
    tokens = mixed_ref.shape[0] - EDGE
    inner = dz_ref.shape[1]
    fill = jnp.zeros((tokens - EDGE, mixed_ref.shape[1]), F32)
    mixed = mixed_ref[EDGE:, :] + jnp.concatenate([fill, next_ref[...]], axis=0)
    x_low = mixed[:, :inner].astype(BF16)
    x_low_ref[...] = x_low
    grad_bc = mixed[:, inner:]
    bc_out_ref[:tokens, :] = grad_bc
    bc_out_ref[tokens:, :] = small_ref[:, inner:]
    high, rest = halves(grad_bc)
    total = (
        dot_low(dz_ref[...], zx_ref[:, :inner], NT)
        + dot_low(x_low, zx_ref[:, inner:], NT)
        + dot_low(high, bc_ref[...], NT)
        + dot_low(rest, bc_ref[...], NT)
        + dot_low(ddt_ref[...], dt_ref[...], NT)
    )
    whole_ref[...] = total
    deal_rows(where_ref, whole_ref, keep_ref, send_ref)


def input_back(where_ref, grad_ref, in_ref, gain_ref, *refs):
    *terms, out_ref, sum_ref, kept_ref = refs
    total = stacked(*terms)
    rows = total.shape[0]

    def half(ref):
        value = ref[half_at(where_ref, 0, rows), :] if ref.shape[0] > rows else ref[...]
        return value.astype(F32)

    block_in = half(in_ref)
    scale = lax.rsqrt(jnp.mean(block_in * block_in, axis=-1, keepdims=True) + EPS)
    weighted = total * gain_ref[...]
    inner_prod = jnp.mean(weighted * block_in, axis=-1, keepdims=True)
    out_ref[...] = (
        half(grad_ref) + scale * weighted - block_in * (scale * scale * scale * inner_prod)
    )
    kept_ref[...] = out_ref[...]
    sum_ref[...] = jnp.broadcast_to(
        jnp.sum(total * block_in * scale, axis=0, keepdims=True), sum_ref.shape
    )


def split_bc(own_ref, got_ref, keep_ref, send_ref):
    total = own_ref[...] + got_ref[...]
    quarter = total.shape[1] // 4
    cols = [total[:, at * quarter : (at + 1) * quarter] for at in range(4)]
    keep_ref[...] = jnp.concatenate([cols[0], cols[2]], axis=1)
    send_ref[...] = jnp.concatenate([cols[1], cols[3]], axis=1)


def narrow_bc(own_ref, got_ref, keep_ref, send_ref):
    total = own_ref[...] + got_ref[...]
    quarter = total.shape[1] // 4
    cols = [total[:, at * quarter : (at + 1) * quarter] for at in range(4)]
    fill = jnp.zeros((total.shape[0], 2 * quarter), F32)
    keep_ref[...] = jnp.concatenate([cols[0], cols[2], fill], axis=1)
    send_ref[...] = jnp.concatenate([cols[1], cols[3], fill], axis=1)


def x_grads(where_ref, n0_ref, n1_ref, x0_ref, x1_ref, keep_ref, send_ref, out_ref, *, rows):
    out_ref[...] = dot_low(n0_ref[...], x0_ref[...], TN) + dot_low(n1_ref[...], x1_ref[...], TN)
    deal_chunks(where_ref, rows, 0, lambda span: out_ref[span, :], keep_ref, send_ref)


def narrow_grads(
    where_ref, half_ref, got_ref, n0_ref, n1_ref, d0_ref, d1_ref, keep_ref, send_ref, rows_ref,
    out_ref, *, pair, rows
):
    total = half_ref[...] + got_ref[...]
    tokens = n0_ref.shape[0]
    low = total[:tokens].astype(BF16)
    rows_ref[...] = total[tokens:]
    normed = jnp.where(where_ref[0] == 0, n0_ref[...].astype(F32), n1_ref[...].astype(F32))
    bc = dot_low(normed, low, TN)
    dt = dot_low(n0_ref[...], d0_ref[...], TN) + dot_low(n1_ref[...], d1_ref[...], TN)
    out_ref[...] = jnp.concatenate([bc[:, :pair], dt[:, : LANES - pair]], axis=1)
    deal_chunks(where_ref, rows, 0, lambda span: out_ref[span, :], keep_ref, send_ref)


def early_grads(
    where_ref, n0_ref, n1_ref, z0_ref, z1_ref, g0_ref, g1_ref, o0_ref, o1_ref, keep_ref, send_ref,
    out_ref, *, rows
):
    inner = z0_ref.shape[1]
    out_ref[:, :inner] = dot_low(n0_ref[...], z0_ref[...], TN) + dot_low(
        n1_ref[...], z1_ref[...], TN
    )
    out_ref[:, inner:] = dot_low(g0_ref[...], o0_ref[...], TN) + dot_low(
        g1_ref[...], o1_ref[...], TN
    )
    deal_chunks(where_ref, rows, 0, lambda span: out_ref[span, :], keep_ref, send_ref)


def sum_rows(bc_ref, *refs, micro):
    small, heads, grow, gains = (refs[at * micro : (at + 1) * micro] for at in range(4))
    out_ref = refs[-1]
    inner = grow[0].shape[1]

    def total(values):
        return functools.reduce(jnp.add, [one[...] for one in values])

    out_ref[...] = jnp.zeros(out_ref.shape, F32)
    out_ref[:EDGE, :inner] = total(small)[:, :inner]
    out_ref[CONV + 1 : CONV + 2, :inner] = total(grow)[:1]
    out_ref[EDGE : 2 * EDGE, :LANES] = total(heads)
    out_ref[EDGE : 2 * EDGE, LANES : 2 * LANES] = bc_ref[...]
    out_ref[CONV + 2 : CONV + 3, :] = total(gains)[:1]


def choose_ends(where_ref, *refs):
    *pieces, send_ref, keep_ref = refs
    micro = len(pieces) // 2
    lower, upper = pieces[:micro], pieces[micro:]

    def write(target_ref, sources):
        for index in range(micro):
            target_ref[index] = sources[index][...]

    @pl.when(where_ref[0] == 0)
    def _():
        write(keep_ref, lower)
        write(send_ref, upper)

    @pl.when(where_ref[0] != 0)
    def _():
        write(keep_ref, upper)
        write(send_ref, lower)


def lay_out(where_ref, own_ref, got_ref, out_ref):
    rows = own_ref.shape[1]
    for index in range(own_ref.shape[0]):
        out_ref[index, half_at(where_ref, 0, rows), :] = own_ref[index]
        out_ref[index, half_at(where_ref, 1, rows), :] = got_ref[index]


def swap(block):
    return lax.ppermute(block, "section", [(0, 1), (1, 0)])


def across(block, mask):
    count = lax.axis_size("head")
    return lax.ppermute(block, "head", [(i, i ^ mask) for i in range(count)])


def along(block, distance):
    devices = range(lax.axis_size("seq"))
    return lax.ppermute(
        block, "seq", [(i, i + distance) for i in devices if i + distance in devices]
    )


def fused(body, *args):
    return kernel_call(body, [(args[0].shape, F32)], args, 0.5, scalars=False)[0]


def carried(own, direction):
    count = lax.axis_size("seq")
    near = along(own, direction)
    yield
    far = jnp.zeros_like(near)
    distance = 2
    while distance < count:
        window = fused(join_window, own, near)
        far = along(window, direction * distance)
        yield
        distance *= 2
        if distance < count:
            near = fused(join_window, near, far)
    return near, far


def sum_all(value):
    got = swap(value)
    yield
    for mask in (1, 2):
        value = fused(add_pair, value, got)
        got = across(value, mask)
        yield
    return value, got


def sum_halves(keep, send):
    got = swap(send)
    yield
    shape = (keep.shape[0] // 2, keep.shape[1])
    first, second = kernel_call(
        add_split, [(shape, F32)] * 2, (keep, got), 0.5, scalars=False
    )
    got_first, got_second = across(first, 1), across(second, 2)
    yield
    first = fused(add_pair, first, got_first)
    got_first = across(first, 2)
    second = fused(add_pair, second, got_second)
    got_second = across(second, 1)
    yield
    return first, got_first, second, got_second


def sum_seq(value):
    count = lax.axis_size("seq")
    got = jnp.zeros_like(value)
    mask = 1
    while mask < count:
        if mask > 1:
            value = fused(add_pair, value, got)
        got = lax.ppermute(value, "seq", [(i, i ^ mask) for i in range(count)])
        yield
        mask *= 2
    return value, got


def on_device(
    inputs, cotangent, in_gain, w_z, w_x, w_bc, w_dt, dt_bias, a_log, skip, conv_x, conv_bc,
    convb_x, convb_bc, norm_gain, w_out
):
    section = lax.axis_index("section")
    parts = lax.axis_size("head")
    where = jnp.stack([section, lax.axis_index("seq")]).astype(jnp.int32)
    micro, tokens, model_w = inputs.shape
    inner = w_z.shape[2] // 2
    heads_n = w_dt.shape[2] // 2
    state_loc = w_bc.shape[3]
    pair = 2 * state_loc
    state_w = state_loc * parts
    channels = inner + 2 * state_w
    rows = tokens // 2
    half = model_w // 2

    pack, send_zx, send_out, own_rows, edge_in = kernel_call(
        pack_weights,
        [((half + EDGE, 2 * pair), F32), ((model_w, 2 * inner), F32), ((inner, model_w), F32),
         ((3 * EDGE, model_w), F32), ((micro, EDGE, model_w), F32)],
        (where, Kept(inputs), Kept(w_z[0]), Kept(w_x[0]), Kept(w_out[0]), Kept(w_bc[0].reshape(model_w, pair)),
         *[
             Kept(one)
             for one in (
                 conv_bc[0].reshape(CONV, pair), convb_bc.reshape(1, pair), w_dt[0], conv_x[0],
                 convb_x, norm_gain, in_gain, dt_bias, a_log, skip,
             )
         ]),
        3, held=True,
    )
    own_packs = [pack] + [across(pack, part) for part in range(1, parts)]
    got_rows = swap(own_rows)
    got_zx = swap(send_zx)
    got_out = swap(send_out)
    halo_in = along(edge_in, 1)
    got_packs = [swap(one) for one in own_packs]
    def weight_outs(*more):
        return [
            ((model_w, 2 * inner), BF16, *more), ((model_w, 2 * state_w), BF16, *more),
            ((model_w, LANES), BF16, *more), ((inner, model_w), BF16, *more),
            ((EDGE, channels), F32, *more), ((EDGE, LANES), F32, *more),
            ((1, inner), F32, *more), ((1, model_w), F32, *more),
        ]

    picked = kernel_call(
        functools.partial(pick_weights, parts=parts),
        weight_outs(True) + weight_outs(True) + weight_outs(),
        (where, Kept(w_z[0]), Kept(w_x[0]), Kept(w_out[0]), got_zx, got_out, own_rows, got_rows,
         *own_packs, *got_packs),
        4,
    )
    blocks = (picked[:8], picked[8:16])
    w_zxs, w_bcs, w_dts, w_outs, taps, head_rows, gains, in_gains = zip(*blocks)
    now = picked[16:]

    project_outs = [
        ((tokens, model_w), BF16, True),
        ((tokens, inner), F32, True),
        ((tokens + EDGE, channels), F32, True),
        ((tokens, channels), F32, True),
        ((tokens, LANES), F32, True),
        ((tokens, LANES), F32, True),
        ((state_w + EDGE, inner), F32, True),
        ((tokens, inner), F32),
        ((tokens, state_w), F32),
        ((tokens, inner), F32),
        ((tokens, inner), F32),
        ((state_w + EDGE, inner), F32),
    ]
    halves_out = [((rows, model_w), F32)] * 2
    whole_scratch = [pltpu.VMEM((tokens, model_w), F32)]

    def summed(sums):
        return fused(add_pair, *sum_heads(fused(add_pair, sums, swap(sums)), 1))

    def forward_first(index):
        *kept, gate, c_ssd, grown, local, state = kernel_call(
            first_forward, project_outs,
            (Kept(inputs, index), halo_in[index], now[7], *now[:3], now[4], now[5]),
            3, scalars=False,
        )
        near, far = yield from carried(state, 1)
        ssd, entry, gated, sums = kernel_call(
            first_output,
            [((tokens, inner), F32, True), ((state_w, inner), F32, True), ((tokens, inner), F32),
             ((EDGE, tokens), F32)],
            (local, near, far, c_ssd, grown, gate), 1, scalars=False,
        )
        sums = yield from sum_all(sums)
        _, keep, send, sums = kernel_call(
            first_branch,
            [((tokens, inner), BF16, True)] + halves_out + [((EDGE, tokens), F32, True)],
            (where, *sums, gated, now[6], now[3]), 2, scratch=whole_scratch,
        )
        terms = yield from sum_halves(keep, send)
        own, own_kept = kernel_call(
            add_base, [((rows, model_w), F32), ((rows, model_w), F32, True)],
            (where, Kept(inputs, index), *terms), 1,
        )
        return (*kept, entry, ssd), own, sums, own_kept

    def forward_second(index, own):
        other = swap(own)
        top = jnp.where(section == 0, other[rows - EDGE :], own[rows - EDGE :])
        halo = along(top, 1)
        yield
        block_in, *kept, gate, c_ssd, grown, local, state = kernel_call(
            later_forward, [((tokens, model_w), F32, True)] + project_outs,
            (where, own, other, halo, in_gains[1], w_zxs[1], w_bcs[1], w_dts[1], taps[1],
             head_rows[1]),
            4,
        )
        near, far = yield from carried(state, 1)
        ssd, entry, grad_norm, sums = kernel_call(
            second_output,
            [((tokens, inner), F32, True), ((state_w, inner), F32, True), ((tokens, inner), F32),
             ((EDGE, tokens), F32)],
            (local, near, far, c_ssd, grown, gate, gains[1], w_outs[1], Kept(cotangent, index)),
            2, scalars=False,
        )
        sums = yield from sum_all(sums)
        return (*kept, entry, ssd), block_in, grad_norm, sums

    gate_outs = [
        ((tokens, inner), F32),
        ((tokens, inner), BF16, True),
        ((tokens, inner), BF16, True),
        ((EDGE, inner), F32, True),
        ((state_w + EDGE, inner), F32),
    ]

    def back_rest(block, kept, dy, dz, grad_entry):
        _, _, pad, conv, dt_val, cum, state, entry, ssd = kept
        near, far = yield from carried(grad_entry, -1)
        mixed, ddt, small, head_sums = kernel_call(
            scan_back,
            [((tokens + EDGE, channels), F32), ((tokens, LANES), BF16, True),
             ((EDGE, channels), F32, True), ((EDGE, LANES), F32, True)],
            (dy, ssd, conv, pad, dt_val, cum, entry, state, near, far, taps[block],
             head_rows[block]),
            4, scratch=[pltpu.VMEM((tokens + 3 * EDGE, channels), F32)], scalars=False, held=True,
        )
        from_next = along(mixed[:EDGE], -1)
        yield
        x_low, grad_bc, keep, send = kernel_call(
            normed_back,
            [((tokens, inner), BF16, True), ((tokens + EDGE, 2 * state_w), F32)] + halves_out,
            (where, mixed, from_next, small, dz, ddt, w_zxs[block], w_bcs[block], w_dts[block]),
            2, scratch=whole_scratch,
        )
        return (x_low, ddt, grad_bc, small, head_sums), keep, send

    def input_grad(block, grad_half, in_half, *terms):
        return kernel_call(
            input_back,
            [((rows, model_w), F32), ((EDGE, model_w), F32, True), ((rows, model_w), F32, True)],
            (where, grad_half, in_half, in_gains[block], *terms), 1,
        )

    shards = lax.axis_size("seq")
    chunk = model_w // shards

    def scattered(keep, send):
        step = 1
        while True:
            mask = 1 << (step - 1)
            pairs = [(i, i ^ mask) for i in range(shards)]
            got = lax.ppermute(send, "seq", pairs)
            yield
            if 2 * mask >= shards:
                return keep, got
            shape = (keep.shape[0] // 2, keep.shape[1])
            keep, send = kernel_call(
                functools.partial(add_chunks, rows=chunk, step=step), [(shape, F32)] * 2,
                (where, keep, got), 0.5,
            )
            step += 1

    def dealt(width):
        return [((model_w // 2, width), F32)] * 2

    def first_grads(normed_all, gates, grads):
        keep, send = kernel_call(
            functools.partial(early_grads, rows=chunk), dealt(2 * inner),
            (where, *normed_all, *[one[1] for one in gates], *grads, *[one[2] for one in gates]),
            3, scratch=[pltpu.VMEM((model_w, 2 * inner), F32)],
        )
        return (yield from scattered(keep, send))

    def second_grads(normed_all, rests):
        keep, send = kernel_call(
            functools.partial(x_grads, rows=chunk), dealt(inner),
            (where, *normed_all, *[one[0] for one in rests]),
            2, scratch=[pltpu.VMEM((model_w, inner), F32)],
        )
        return (yield from scattered(keep, send))

    def third_grads(normed_all, rests, block):
        ddt, grad_bc = ([one[at] for one in rests] for at in (1, 2))
        shape = (grad_bc[0].shape, F32)
        own, other = kernel_call(pick_pair, [shape] * 2, (where, *grad_bc), 0.5)
        got = swap(other)
        yield
        thin = [((tokens + EDGE, 2 * pair), F32)] * 2
        keep, send = kernel_call(split_bc, thin, (own, got), 0.5, scalars=False)
        got = across(send, 1)
        yield
        keep, send = kernel_call(narrow_bc, thin, (keep, got), 0.5, scalars=False)
        got = across(send, 2)
        yield
        keep, send, bc_rows = kernel_call(
            functools.partial(narrow_grads, pair=pair, rows=chunk),
            dealt(LANES) + [((EDGE, LANES), F32, True)],
            (where, keep, got, *normed_all, *ddt), 2,
            scratch=[pltpu.VMEM((model_w, LANES), F32)],
        )
        found["bc", block] = bc_rows
        return (yield from scattered(keep, send))

    def row_sums(bc_rows, rests, grow_all, gain_all):
        (total,) = kernel_call(
            functools.partial(sum_rows, micro=micro), [((2 * EDGE, model_w), F32)],
            (bc_rows, *[one[3] for one in rests], *[one[4] for one in rests], *grow_all,
             *gain_all),
            0.5, scalars=False,
        )
        return (yield from sum_seq(total))

    each = range(micro)
    both = tuple("m%d" % index for index in each)
    first = [None] * micro
    second = [None] * micro
    gates = [[None] * micro, [None] * micro]
    rests = [[None] * micro, [None] * micro]
    mids = [None] * micro
    lasts = [None] * micro
    upper = [None] * micro
    lows = [None] * micro

    def chain(index):
        first[index] = yield from forward_first(index)
        second[index] = yield from forward_second(index, first[index][1])
        kept, block_in, grad_norm, sums = second[index]
        gates[1][index] = kernel_call(
            second_gate, gate_outs,
            (*sums, grad_norm, kept[8], kept[1], gains[1], kept[3], kept[5], kept[6]),
            2, scalars=False,
        )
        dy, dz, _, _, grad_entry = gates[1][index]
        rests[1][index], keep, send = yield from back_rest(1, kept, dy, dz, grad_entry)
        terms = yield from sum_halves(keep, send)
        mids[index] = input_grad(1, Kept(cotangent, index), first[index][3], *terms)
        own = mids[index][0]
        other = swap(own)
        yield
        kept = first[index][0]
        lows[index], *gates[0][index] = kernel_call(
            first_gate, [((tokens, model_w), BF16, True)] + gate_outs,
            (where, own, other, block_in, Kept(inputs, index), first[index][2], w_outs[0],
             kept[8], kept[1], gains[0], kept[3], kept[5], kept[6]),
            3, scratch=whole_scratch,
        )
        dy, dz, _, _, grad_entry = gates[0][index]
        rests[0][index], keep, send = yield from back_rest(0, kept, dy, dz, grad_entry)
        terms = yield from sum_halves(keep, send)
        lasts[index] = input_grad(0, mids[index][2], Kept(inputs, index), *terms)

    def top_output(index):
        until(full(gates[1]), *both)
        keep, send = kernel_call(
            out_project, halves_out, (where, gates[1][index][2], w_outs[1]), 1,
            scratch=whole_scratch,
        )
        terms = yield from sum_halves(keep, send)
        upper[index] = kernel_call(
            add_base, [((rows, model_w), F32, True)] * 2, (where, first[index][3], *terms), 1
        )

    found = {}

    def normed_of(block):
        return [one[0][0] for one in (first, second)[block]]

    def until(ready, *names):
        while not ready():
            for name in names:
                next(chains[name], None)

    def full(values):
        return lambda: all(value is not None for value in values)

    def part(name, block):
        if name == "early":
            until(full(gates[block]), *both)
        elif name == "rows":
            until(lambda: ("bc", block) in found, "narrow%d" % block)
            until(full((lasts, mids)[block]), *both)
        else:
            until(full(rests[block]), *both)
        if name == "early":
            grads = lows if block == 0 else [Kept(cotangent, index) for index in each]
            found[name, block] = yield from first_grads(normed_of(block), gates[block], grads)
        elif name == "wide":
            found[name, block] = yield from second_grads(normed_of(block), rests[block])
        elif name == "narrow":
            found[name, block] = yield from third_grads(
                normed_of(block), rests[block], block
            )
        else:
            gain_all = [one[1] for one in (lasts, mids)[block]]
            found[name, block] = yield from row_sums(
                found["bc", block], rests[block], [one[3] for one in gates[block]],
                gain_all,
            )

    def trade(name):
        if name == "ends":
            until(full(lasts), *both)
            until(full(upper), "u0", "u%d" % (micro - 1))
            shape = (micro, rows, model_w)
            send, keep = kernel_call(
                choose_ends, [(shape, F32), (shape, F32)],
                (where, *[one[0] for one in lasts], *[one[0] for one in upper]), 1,
            )
        else:
            for block in (0, 1):
                until(lambda: (name, block) in found, "%s%d" % (name, block))
            low_one, top_one = found[name, 0], found[name, 1]
            shape = low_one[0].shape
            keep, send = kernel_call(
                pick_sums, [(shape, F32), (shape, F32)], (where, *low_one, *top_one), 0.5
            )
        found["trade", name] = keep, swap(send)
        yield

    chains = {"m%d" % index: chain(index) for index in each}
    chains.update({"u%d" % index: top_output(index) for index in each})
    chains.update({"t" + name: trade(name) for name in ("early", "wide", "narrow", "rows", "ends")})
    for block in (0, 1):
        for name in ("early", "wide", "narrow", "rows"):
            chains["%s%d" % (name, block)] = part(name, block)

    def run(*names):
        for name in names:
            next(chains[name], None)

    while gates[1][-1] is None:
        run(*both)
    a, b = both[0], both[-1]
    for names in SCHEDULE:
        run(*[{"a": a, "b": b}.get(name, name) for name in names])
    for name in ("tearly", "twide", "tnarrow", "trows", "tends"):
        for _ in chains[name]:
            pass
    (ends,) = kernel_call(
        lay_out, [((micro, tokens, model_w), F32, True)], (where, *found["trade", "ends"]), 1
    )
    size = chunk
    own, got = found["trade", "early"]
    g_w_z, g_w_out = kernel_call(
        join_first, [((size, 2 * inner), F32, True), ((2 * inner, size), F32, True)],
        (where, own, got), 1,
    )
    own, got = found["trade", "wide"]
    (g_w_x,) = kernel_call(join_second, [((size, 2 * inner), F32, True)], (where, own, got), 1)
    own, got = found["trade", "narrow"]
    narrow, own_dt, got_dt = own + got, own, got
    g_w_bc = narrow[:, :pair].reshape(-1, 2, state_loc)
    mine = section == 0

    def both_sides(own, got):
        return jnp.concatenate([jnp.where(mine, own, got), jnp.where(mine, got, own)], axis=1)

    g_w_dt = both_sides(own_dt[:, pair : pair + heads_n], got_dt[:, pair : pair + heads_n])
    own, got = found["trade", "rows"]
    shapes = [
        (CONV, 2 * inner), (1, 2 * inner), (1, 2 * inner), (1, model_w), (1, 2 * heads_n),
        (1, 2 * heads_n), (1, 2 * heads_n), (EDGE, pair),
    ]
    *row_set, bc_set = (
        one.value
        for one in kernel_call(
            join_rows, [(shape, F32, True) for shape in shapes], (where, own, got), 0.5
        )
    )
    g_conv_x, g_convb_x, g_norm_gain, g_in_gain, g_bias, g_log, g_skip = row_set
    return (
        ends.value[None],
        g_in_gain,
        g_w_z.value[None],
        g_w_x.value[None],
        g_w_bc[None],
        g_w_dt[None],
        g_bias,
        g_log,
        g_skip,
        g_conv_x[None],
        bc_set[:CONV].reshape(1, CONV, 2, state_loc),
        g_convb_x,
        bc_set[CONV : CONV + 1].reshape(1, 2, state_loc),
        g_norm_gain,
        g_w_out.value[None],
    )


def solution(mesh):
    Line.mark = None
    in_specs = (
        P(None, "seq", None),
        P(None, "seq", None),
        P("section", None),
        P("section", None, "head"),
        P("section", None, "head"),
        P("section", None, None, "head"),
        P("section", None, "head"),
        P("section", "head"),
        P("section", "head"),
        P("section", "head"),
        P("section", None, "head"),
        P("section", None, None, "head"),
        P("section", "head"),
        P("section", None, "head"),
        P("section", "head"),
        P("section", "head", None),
    )
    out_specs = (
        P("section", None, "seq", None),
        P("section", None),
        P("section", "seq", "head"),
        P("section", "seq", "head"),
        P("section", "seq", None, "head"),
        P("section", "seq", "head"),
        P("section", "head"),
        P("section", "head"),
        P("section", "head"),
        P("section", None, "head"),
        P("section", None, None, "head"),
        P("section", "head"),
        P("section", None, "head"),
        P("section", "head"),
        P("section", "head", "seq"),
    )
    return jax.shard_map(
        on_device, mesh=mesh, in_specs=in_specs, out_specs=out_specs, check_vma=False
    )
```

```python
import functools

import jax
import jax.numpy as jnp
from jax import lax
from jax.experimental import pallas as pl
from jax.experimental.pallas import tpu as pltpu
from jax.sharding import PartitionSpec as P

ED = 2048
HEAD = 64
CONV = 4
EPS = 1e-05
EDGE = 8
LANES = 128
VMEM_LIMIT = 20 * 1024 * 1024
F32 = jnp.float32
BF16 = jnp.bfloat16
NN = (((1,), (0,)), ((), ()))
NT = (((1,), (1,)), ((), ()))
TN = (((0,), (0,)), ((), ()))


SCHEDULE = (
    ("a", "b", "u0", "u1"),
    ("a", "u0", "b", "u1"),
    ("a", "u0", "b", "u1", "early1"),
    ("a", "u0", "b", "u1"),
    ("a", "b", "wide1", "narrow1"),
    ("a", "b", "early1", "narrow1"),
    ("a", "b", "narrow1", "narrow1"),
    ("a", "b", "early0"),
    ("a", "b", "wide1", "narrow1", "rows1"),
    ("a", "wide1", "narrow1", "b"),
    ("a", "b", "wide0", "narrow0"),
    ("a", "b", "narrow0", "early0", "rows1"),
    ("a", "b", "narrow0", "wide0", "narrow0"),
    ("tends", "early0", "tearly"),
    ("narrow0", "rows0", "wide0", "twide"),
    ("rows0", "narrow0", "tnarrow", "rows0", "trows"),
)


def dot_low(left, right, dims=NN):
    return lax.dot_general(left.astype(BF16), right.astype(BF16), dims, preferred_element_type=F32)


def halves(value):
    high = value.astype(BF16)
    return high, (value - high.astype(F32)).astype(BF16)


def dot_split(left, right, dims=NN):
    left_hi, left_lo = halves(left)
    right_hi, right_lo = halves(right)
    mul = functools.partial(lax.dot_general, dimension_numbers=dims, preferred_element_type=F32)
    return mul(left_hi, right_hi) + (mul(left_hi, right_lo) + mul(left_lo, right_hi))


def dot_exact(left, right, dims=NN):
    return lax.dot_general(
        left, right, dims, precision=lax.Precision.HIGHEST, preferred_element_type=F32
    )


dot_mix = dot_split
dot_sum = dot_exact


class Line:
    mark = None


class Kept:
    def __init__(self, value, index=None):
        self.value = value
        self.index = index


def kernel_call(body, outs, args, time_us, scratch=(), scalars=True, held=False):
    whole = pl.BlockSpec(memory_space=pltpu.VMEM)
    specs = []
    values = []
    for at, arg in enumerate(args):
        if scalars and at == 0:
            specs.append(pl.BlockSpec(memory_space=pltpu.SMEM))
            values.append(arg)
        elif isinstance(arg, Kept):
            value = arg.value
            if held:
                value = pltpu.with_memory_space_constraint(value, pltpu.HBM)
            values.append(value)
            specs.append(whole)
        else:
            values.append(pltpu.with_memory_space_constraint(arg, pltpu.VMEM))
            specs.append(whole)
    places = [arg.index if isinstance(arg, Kept) else None for arg in args]
    before = [] if Line.mark is None else [Line.mark]
    specs.extend([pl.BlockSpec(memory_space=pl.ANY)] * len(before))
    inputs_n = len(args) + len(before)

    def viewed(*refs):
        views = [
            ref if at is None else ref.at[at] for ref, at in zip(refs, places)
        ]
        refs[inputs_n][...] = jnp.zeros((EDGE, LANES), F32)
        body(*views, *refs[inputs_n + 1 :])

    results = pl.pallas_call(
        viewed,
        out_shape=[pltpu.VMEM((EDGE, LANES), F32)]
        + [(pltpu.HBM if len(out) > 2 else pltpu.VMEM)(out[0], out[1]) for out in outs],
        in_specs=specs,
        out_specs=[whole] * (1 + len(outs)),
        scratch_shapes=list(scratch),
        compiler_params=pltpu.CompilerParams(vmem_limit_bytes=VMEM_LIMIT),
        cost_estimate=pl.CostEstimate(
            flops=0, bytes_accessed=int(time_us * 3_000_000), transcendentals=0
        ),
    )(*values, *before)
    Line.mark, *results = results
    return [
        Kept(result) if len(out) > 2 else result for out, result in zip(outs, results)
    ]


def sigmoid(values):
    return 1.0 / (1.0 + jnp.exp(-values))


def softplus(values):
    return jnp.maximum(values, 0.0) + jnp.log1p(jnp.exp(-jnp.abs(values)))


def one_hot(channels):
    head_of = lax.broadcasted_iota(jnp.int32, (channels, LANES), 0) // HEAD
    return (head_of == lax.broadcasted_iota(jnp.int32, (channels, LANES), 1)).astype(F32)


def spread(per_head, channels):
    rows = per_head.shape[0]
    return jnp.concatenate(
        [
            jnp.broadcast_to(per_head[:, head : head + 1], (rows, HEAD))
            for head in range(channels // HEAD)
        ],
        axis=1,
    )


def ordered(tokens):
    row = lax.broadcasted_iota(jnp.int32, (tokens, tokens), 0)
    col = lax.broadcasted_iota(jnp.int32, (tokens, tokens), 1)
    return row >= col


def half_at(where_ref, side, rows):
    start = (where_ref[0] if side == 0 else 1 - where_ref[0]) * rows
    return pl.ds(pl.multiple_of(start, rows), rows)


def gather_rows(where_ref, target_ref, own_ref, other_ref):
    rows = own_ref.shape[0]
    target_ref[half_at(where_ref, 0, rows), :] = own_ref[...]
    target_ref[half_at(where_ref, 1, rows), :] = other_ref[...]


def deal_rows(where_ref, source_ref, keep_ref, send_ref):
    rows = keep_ref.shape[0]
    keep_ref[...] = source_ref[half_at(where_ref, 0, rows), :]
    send_ref[...] = source_ref[half_at(where_ref, 1, rows), :]


def deal_chunks(where_ref, rows, step, read, keep_ref, send_ref):
    bit = jnp.bitwise_and(lax.shift_right_logical(where_ref[1], step), 1)
    for at in range(keep_ref.shape[0] // rows):
        span = slice(at * rows, (at + 1) * rows)
        start = pl.multiple_of((2 * at + bit) * rows, rows)
        keep_ref[span, :] = read(pl.ds(start, rows))
        start = pl.multiple_of((2 * at + 1 - bit) * rows, rows)
        send_ref[span, :] = read(pl.ds(start, rows))


def add_chunks(where_ref, left_ref, right_ref, keep_ref, send_ref, *, rows, step):
    deal_chunks(
        where_ref, rows, step, lambda span: left_ref[span, :] + right_ref[span, :], keep_ref,
        send_ref,
    )


def add_pair(left_ref, right_ref, out_ref):
    out_ref[...] = left_ref[...] + right_ref[...]


def pick_pair(where_ref, first_ref, second_ref, own_ref, other_ref):
    @pl.when(where_ref[0] == 0)
    def _():
        own_ref[...] = first_ref[...]
        other_ref[...] = second_ref[...]

    @pl.when(where_ref[0] != 0)
    def _():
        own_ref[...] = second_ref[...]
        other_ref[...] = first_ref[...]


def pick_sums(where_ref, low_ref, low_got_ref, top_ref, top_got_ref, own_ref, other_ref):
    low = low_ref[...] + low_got_ref[...]
    top = top_ref[...] + top_got_ref[...]
    own_ref[...] = jnp.where(where_ref[0] == 0, low, top)
    other_ref[...] = jnp.where(where_ref[0] == 0, top, low)


def join_sides(where_ref, own, got, axis):
    first = jnp.where(where_ref[0] == 0, own, got)
    second = jnp.where(where_ref[0] == 0, got, own)
    return jnp.concatenate([first, second], axis=axis)


def join_first(where_ref, own_ref, got_ref, z_ref, out_ref):
    width = own_ref.shape[1] // 2
    z_ref[...] = join_sides(where_ref, own_ref[:, :width], got_ref[:, :width], 1)
    out_ref[...] = join_sides(where_ref, own_ref[:, width:].T, got_ref[:, width:].T, 0)


def join_second(where_ref, own_ref, got_ref, x_ref):
    x_ref[...] = join_sides(where_ref, own_ref[...], got_ref[...], 1)


def join_rows(
    where_ref, own_ref, got_ref, conv_ref, convb_ref, norm_ref, gain_ref, bias_ref, log_ref,
    skip_ref, bc_ref
):
    own = own_ref[...]
    got = got_ref[...]
    inner = conv_ref.shape[1] // 2
    heads_n = bias_ref.shape[1] // 2
    both = join_sides(where_ref, own[:EDGE, :inner], got[:EDGE, :inner], 1)
    conv_ref[...] = both[:CONV]
    convb_ref[...] = both[CONV : CONV + 1]
    norm_ref[...] = both[CONV + 1 : CONV + 2]
    total = own + got
    gain_ref[...] = total[CONV + 2 : CONV + 3]
    heads = join_sides(where_ref, own[EDGE:, :heads_n], got[EDGE:, :heads_n], 1)
    bias_ref[...] = heads[0:1]
    log_ref[...] = heads[1:2]
    skip_ref[...] = heads[2:3]
    bc_ref[...] = total[EDGE:, LANES : LANES + bc_ref.shape[1]]


def join_window(own_ref, near_ref, window_ref):
    depth = own_ref.shape[0] - EDGE
    decay = own_ref[depth : depth + 1, :]
    window_ref[:depth, :] = own_ref[:depth, :] + jnp.exp(decay) * near_ref[:depth, :]
    window_ref[depth:, :] = own_ref[depth:, :] + near_ref[depth:, :]


def pack_weights(
    where_ref, in_ref, z_ref, x_ref, out_ref, bc_ref, conv_bc_ref, convb_bc_ref, dt_ref, conv_x_ref,
    convb_x_ref, gain_ref, in_gain_ref, bias_ref, log_ref, skip_ref,
    pack_ref, send_zx_ref, send_out_ref, rows_ref, edge_ref
):
    edge_ref[...] = in_ref[:, in_ref.shape[1] - EDGE :, :].astype(F32)
    model_w, width = z_ref.shape
    inner = width // 2
    half = model_w // 2
    pair = bc_ref.shape[1]
    there = half_at(where_ref, 1, inner)
    pack_ref[:half, :pair] = bc_ref[:half, :].astype(F32)
    pack_ref[:half, pair:] = bc_ref[half:, :].astype(F32)
    pack_ref[half:, :] = jnp.zeros((EDGE, 2 * pair), F32)
    pack_ref[half : half + CONV, :pair] = conv_bc_ref[...]
    pack_ref[half + CONV : half + CONV + 1, :pair] = convb_bc_ref[...]
    send_zx_ref[:, :inner] = z_ref[:, there].astype(F32)
    send_zx_ref[:, inner:] = x_ref[:, there].astype(F32)
    send_out_ref[...] = out_ref[there, :].astype(F32)
    heads_n = dt_ref.shape[1]
    rows_ref[...] = jnp.zeros(rows_ref.shape, F32)
    rows_ref[:CONV, :width] = conv_x_ref[...]
    rows_ref[CONV : CONV + 1, :width] = convb_x_ref[...]
    rows_ref[CONV + 1 : CONV + 2, :width] = gain_ref[...]
    rows_ref[CONV + 2 : CONV + 3, :] = in_gain_ref[...]
    rows_ref[EDGE : EDGE + 1, :heads_n] = bias_ref[...]
    rows_ref[EDGE + 1 : EDGE + 2, :heads_n] = log_ref[...]
    rows_ref[EDGE + 2 : EDGE + 3, :heads_n] = skip_ref[...]
    rows_ref[2 * EDGE : 2 * EDGE + heads_n, :] = dt_ref[...].astype(F32).T


def pick_weights(
    where_ref, z_ref, x_ref, out_ref, got_zx_ref, got_out_ref, own_rows_ref, got_rows_ref,
    *refs, parts
):
    own_packs, got_packs, outs = refs[:parts], refs[parts : 2 * parts], refs[2 * parts :]
    section = where_ref[0]
    model_w = z_ref.shape[0]
    half = model_w // 2
    inner = got_zx_ref.shape[1] // 2
    pair = own_packs[0].shape[1] // 2
    heads_n = inner // HEAD
    here = half_at(where_ref, 0, inner)

    def side(value):
        return jnp.where(section == 0, value[:, :inner], value[:, inner : 2 * inner])

    def write(refs, zx, out_part, packs, rows_ref):
        zx_to, bc_to, dt_to, out_to, taps_to, heads_to, gain_to, in_to = refs
        zx_to[:, :inner] = zx[0]
        zx_to[:, inner:] = zx[1]
        out_to[...] = out_part
        loc = pair // 2
        order = [0, 2, 1, 3] if parts == 4 else list(range(parts))
        values = [packs[part][...] for part in order]

        def columns(low, top):
            return jnp.concatenate(
                [one[low:top, :loc] for one in values]
                + [one[low:top, loc:pair] for one in values],
                axis=1,
            )

        bc_to[:half, :] = columns(0, half).astype(BF16)
        bc_to[half:, :] = jnp.concatenate(
            [one[:half, pair : pair + loc] for one in values]
            + [one[:half, pair + loc :] for one in values],
            axis=1,
        ).astype(BF16)
        rows = rows_ref[...]
        taps_to[:, :inner] = side(rows[:EDGE])
        taps_to[:, inner:] = columns(half, half + EDGE)
        gain_to[...] = side(rows[CONV + 1 : CONV + 2])
        in_to[...] = rows[CONV + 2 : CONV + 3]
        lane = lax.broadcasted_iota(jnp.int32, (EDGE, LANES), 1)
        vecs = rows[EDGE : 2 * EDGE, :LANES]
        vecs = jnp.where(section == 0, vecs, pltpu.roll(vecs, LANES - heads_n, 1))
        heads_to[...] = jnp.where(lane < heads_n, vecs, 0.0)
        dt_rows = rows[2 * EDGE :]
        dt_rows = jnp.where(
            section == 0,
            dt_rows[:heads_n],
            dt_rows[heads_n : 2 * heads_n],
        )
        fill = jnp.zeros((LANES - heads_n, model_w), F32)
        dt_to[...] = jnp.concatenate([dt_rows, fill], axis=0).T.astype(BF16)

    own = ((z_ref[:, here], x_ref[:, here]), out_ref[here, :], own_packs, own_rows_ref)
    got = (
        (got_zx_ref[:, :inner].astype(BF16), got_zx_ref[:, inner:].astype(BF16)),
        got_out_ref[...].astype(BF16), got_packs, got_rows_ref,
    )
    first, second, now = outs[:8], outs[8:16], outs[16:]

    @pl.when(section == 0)
    def _():
        write(first, *own)
        write(now, *own)
        write(second, *got)

    @pl.when(section != 0)
    def _():
        write(first, *got)
        write(now, *got)
        write(second, *own)


def project(block_in, halo, in_gain, w_zx, w_bc, w_dt, taps, heads, outs):
    normed_ref, gate_ref, pad_ref, conv_ref, dt_ref, cum_ref, state_ref, *soon = outs
    gate_now_ref, c_now_ref, grown_ref, local_ref, state_now_ref = soon
    tokens = block_in.shape[0]
    inner = w_zx.shape[1] // 2
    rows = jnp.concatenate([halo, block_in], axis=0)
    scale = lax.rsqrt(jnp.mean(rows * rows, axis=-1, keepdims=True) + EPS)
    normed = (rows * scale * in_gain).astype(BF16)
    low = normed[EDGE:]
    normed_ref[...] = low
    gate = dot_low(low, w_zx[:, :inner])
    gate_ref[...] = gate
    gate_now_ref[...] = gate * sigmoid(gate)
    pad_ref[:, :inner] = dot_low(normed, w_zx[:, inner:])
    pad_ref[:, inner:] = dot_low(normed, w_bc)
    dt_val = dot_low(low, w_dt) + heads[0:1, :]
    dt_ref[...] = dt_val
    conv = taps[CONV : CONV + 1, :]
    for tap in range(CONV):
        first = EDGE - CONV + 1 + tap
        conv = conv + taps[tap : tap + 1, :] * pad_ref[first : first + tokens, :]
    conv_ref[...] = conv
    act = conv * sigmoid(conv)
    state_w = (act.shape[1] - inner) // 2
    x_ssd = act[:, :inner]
    b_ssd = act[:, inner : inner + state_w]
    c_ssd = act[:, inner + state_w :]
    c_now_ref[...] = c_ssd
    log_rate = -jnp.exp(heads[1:2, :])
    step = softplus(dt_val)
    lower = ordered(tokens)
    cum = dot_sum(lower.astype(F32), step * log_rate)
    cum_ref[...] = cum
    cum_rows = cum.T
    scaled = x_ssd * spread(step, inner)
    cross = jnp.where(lower, dot_mix(c_ssd, b_ssd, NT), 0.0)
    outputs = []
    for head in range(inner // HEAD):
        gap = cum[:, head : head + 1] - cum_rows[head : head + 1, :]
        mix = cross * jnp.exp(jnp.minimum(gap, 0.0))
        outputs.append(dot_mix(mix, scaled[:, head * HEAD : (head + 1) * HEAD]))
    local_ref[...] = jnp.concatenate(outputs, axis=1) + spread(heads[2:3, :], inner) * x_ssd
    cum_chan = spread(cum, inner)
    last = cum_chan[tokens - 1 : tokens, :]
    grown_ref[...] = jnp.exp(cum_chan)
    state_now_ref[:state_w, :] = dot_mix(b_ssd, scaled * jnp.exp(last - cum_chan), TN)
    state_now_ref[state_w:, :] = jnp.broadcast_to(last, (EDGE, inner))
    state_ref[...] = state_now_ref[...]


def first_forward(in_ref, halo_ref, gain_ref, zx_ref, bc_ref, dt_ref, taps_ref, heads_ref, *outs):
    project(
        in_ref[...].astype(F32), halo_ref[...], gain_ref[...], zx_ref[...], bc_ref[...],
        dt_ref[...], taps_ref[...], heads_ref[...], outs,
    )


def later_forward(
    where_ref, own_ref, other_ref, halo_ref, gain_ref, zx_ref, bc_ref, dt_ref, taps_ref,
    heads_ref, in_ref, *outs
):
    gather_rows(where_ref, in_ref, own_ref, other_ref)
    project(
        in_ref[...], halo_ref[...], gain_ref[...], zx_ref[...], bc_ref[...], dt_ref[...],
        taps_ref[...], heads_ref[...], outs,
    )


def entered(near, far):
    depth = near.shape[0] - EDGE
    return near[:depth] + jnp.exp(near[depth : depth + 1]) * far[:depth]


def mixed_output(local_ref, near_ref, far_ref, c_ref, grown_ref, gate_ref, entry_ref):
    entry = entered(near_ref[...], far_ref[...])
    entry_ref[...] = entry
    ssd = local_ref[...] + grown_ref[...] * dot_mix(c_ref[...], entry)
    return ssd, ssd * gate_ref[...]


def sums_of(squares, inner_prod):
    lane = lax.broadcasted_iota(jnp.int32, (squares.shape[0], LANES), 1)
    both = jnp.where(lane == 0, squares, jnp.where(lane == 1, inner_prod, 0.0))
    return both.T[:EDGE, :]


def rate_of(sums):
    fill = jnp.zeros((LANES - sums.shape[0], sums.shape[1]), F32)
    columns = jnp.concatenate([sums, fill], axis=0).T
    return lax.rsqrt(columns[:, :1] / ED + EPS), columns[:, 1:2]


def first_output(
    local_ref, near_ref, far_ref, c_ref, grown_ref, gate_ref,
    ssd_ref, entry_ref, gated_ref, sums_ref
):
    ssd, gated = mixed_output(
        local_ref, near_ref, far_ref, c_ref, grown_ref, gate_ref, entry_ref
    )
    ssd_ref[...] = ssd
    gated_ref[...] = gated
    sums_ref[...] = sums_of(jnp.sum(gated * gated, axis=-1, keepdims=True), 0.0)


def first_branch(
    where_ref, sums_ref, more_ref, gated_ref, gain_ref, w_out_ref, norm_ref, keep_ref, send_ref,
    sums_out_ref, whole_ref
):
    sums = sums_ref[...] + more_ref[...]
    rate, _ = rate_of(sums)
    sums_out_ref[...] = sums
    norm_out = (gated_ref[...] * rate * gain_ref[...]).astype(BF16)
    norm_ref[...] = norm_out
    whole_ref[...] = dot_low(norm_out, w_out_ref[...])
    deal_rows(where_ref, whole_ref, keep_ref, send_ref)


def second_output(
    local_ref, near_ref, far_ref, c_ref, grown_ref, gate_ref, gain_ref, w_out_ref, cot_ref,
    ssd_ref, entry_ref, grad_norm_ref, sums_ref
):
    ssd, gated = mixed_output(
        local_ref, near_ref, far_ref, c_ref, grown_ref, gate_ref, entry_ref
    )
    ssd_ref[...] = ssd
    grad_norm = dot_low(cot_ref[...], w_out_ref[...], NT)
    grad_norm_ref[...] = grad_norm
    squares = jnp.sum(gated * gated, axis=-1, keepdims=True)
    inner_prod = jnp.sum(grad_norm * gain_ref[...] * gated, axis=-1, keepdims=True)
    sums_ref[...] = sums_of(squares, inner_prod)


def add_split(left_ref, right_ref, first_ref, second_ref):
    rows = first_ref.shape[0]
    first_ref[...] = left_ref[:rows, :] + right_ref[:rows, :]
    second_ref[...] = left_ref[rows:, :] + right_ref[rows:, :]


def stacked(own_first, got_first, own_second, got_second):
    return jnp.concatenate(
        [own_first[...] + got_first[...], own_second[...] + got_second[...]], axis=0
    )


def add_base(where_ref, base_ref, *refs):
    *terms, out_ref, kept_ref = refs
    rows = out_ref.shape[0]
    base = base_ref[half_at(where_ref, 0, rows), :] if base_ref.shape[0] > rows else base_ref[...]
    total = base.astype(F32) + stacked(*terms)
    out_ref[...] = total
    kept_ref[...] = total


def gate_back(grad_norm, rate, cross, ssd, gate, gain, conv, cum, state, outs):
    dy_ref, dz_ref, norm_ref, grow_ref, entry_ref = outs
    inner = ssd.shape[1]
    state_w = (conv.shape[1] - inner) // 2
    sig = sigmoid(gate)
    silu = gate * sig
    gated = ssd * silu
    unit = gated * rate
    norm_ref[...] = (unit * gain).astype(BF16)
    grow_ref[...] = jnp.broadcast_to(
        jnp.sum(grad_norm * unit, axis=0, keepdims=True), (EDGE, inner)
    )
    grad_gated = rate * (grad_norm * gain) - unit * (rate * rate * cross / ED)
    dy = grad_gated * silu
    dy_ref[...] = dy
    dz_ref[...] = (grad_gated * ssd * (sig * (1.0 + gate * (1.0 - sig)))).astype(BF16)
    conv_c = conv[:, inner + state_w :]
    c_ssd = conv_c * sigmoid(conv_c)
    grown = jnp.exp(spread(cum, inner))
    entry_ref[:state_w, :] = dot_mix(c_ssd, grown * dy, TN)
    entry_ref[state_w:, :] = state[state_w:, :]


def second_gate(
    sums_ref, more_ref, grad_norm_ref, ssd_ref, gate_ref, gain_ref, conv_ref, cum_ref, state_ref, *outs
):
    rate, cross = rate_of(sums_ref[...] + more_ref[...])
    gate_back(
        grad_norm_ref[...], rate, cross, ssd_ref[...], gate_ref[...], gain_ref[...],
        conv_ref[...], cum_ref[...], state_ref[...], outs,
    )


def first_gate(
    where_ref, own_ref, other_ref, after_ref, before_ref, sums_ref, w_out_ref, ssd_ref,
    gate_ref, gain_ref, conv_ref, cum_ref, state_ref, low_ref, *outs
):
    *outs, whole_ref = outs
    gather_rows(where_ref, whole_ref, own_ref, other_ref)
    grad_low = whole_ref[...].astype(BF16)
    low_ref[...] = grad_low
    grad_norm = dot_low(grad_low, w_out_ref[...], NT)
    rate, _ = rate_of(sums_ref[...])
    branch = after_ref[...] - before_ref[...].astype(F32)
    cross = jnp.sum(grad_low.astype(F32) * branch, axis=-1, keepdims=True) / rate
    gate_back(
        grad_norm, rate, cross, ssd_ref[...], gate_ref[...], gain_ref[...], conv_ref[...],
        cum_ref[...], state_ref[...], outs,
    )


def out_project(where_ref, norm_ref, w_out_ref, keep_ref, send_ref, whole_ref):
    whole_ref[...] = dot_low(norm_ref[...], w_out_ref[...])
    deal_rows(where_ref, whole_ref, keep_ref, send_ref)


def scan_back(
    dy_ref, ssd_ref, conv_ref, pad_ref, dt_ref, cum_ref, entry_ref, state_ref, near_ref, far_ref,
    taps_ref, heads_ref, mixed_ref, ddt_ref, small_ref, heads_out_ref, line_ref
):
    tokens, inner = dy_ref.shape
    state_w = entry_ref.shape[0]
    dy = dy_ref[...]
    conv = conv_ref[...]
    sig = sigmoid(conv)
    act = conv * sig
    x_ssd = act[:, :inner]
    b_ssd = act[:, inner : inner + state_w]
    c_ssd = act[:, inner + state_w :]
    heads = heads_ref[...]
    log_rate = -jnp.exp(heads[1:2, :])
    skip = spread(heads[2:3, :], inner)
    dt_val = dt_ref[...]
    step = softplus(dt_val)
    cum = cum_ref[...]
    cum_rows = cum.T
    cum_chan = spread(cum, inner)
    step_chan = spread(step, inner)
    last = cum_chan[tokens - 1 : tokens, :]
    tail = jnp.exp(last - cum_chan)
    scaled = x_ssd * step_chan
    entry = entry_ref[...]
    later = entered(near_ref[...], far_ref[...])
    lower = ordered(tokens)
    cross = jnp.where(lower, dot_mix(c_ssd, b_ssd, NT), 0.0)
    grad_cross = jnp.zeros((tokens, tokens), F32)
    grad_scaled = []
    for head in range(inner // HEAD):
        span = slice(head * HEAD, (head + 1) * HEAD)
        gap = cum[:, head : head + 1] - cum_rows[head : head + 1, :]
        decay = jnp.exp(jnp.minimum(gap, 0.0))
        grad_scaled.append(dot_mix(cross * decay, dy[:, span], TN))
        grad_cross = grad_cross + decay * dot_mix(dy[:, span], scaled[:, span], NT)
    grad_cross = jnp.where(lower, grad_cross, 0.0)
    grad_scaled = jnp.concatenate(grad_scaled, axis=1) + tail * dot_mix(b_ssd, later)
    grad_c = dot_mix(grad_cross, b_ssd) + dot_mix(jnp.exp(cum_chan) * dy, entry, NT)
    grad_b = dot_mix(grad_cross, c_ssd, TN) + dot_mix(tail * scaled, later, NT)
    grad_x = step_chan * grad_scaled + skip * dy
    hot = one_hot(inner)
    dx_prod = x_ssd * grad_scaled
    dy_x = dy * x_ssd
    grad_cum = dot_sum(dy * ssd_ref[...] - skip * dy_x - step_chan * dx_prod, hot)
    final = jnp.exp(last) * entry + state_ref[:state_w, :]
    at_end = jnp.broadcast_to(jnp.sum(later * final, axis=0, keepdims=True), (EDGE, inner))
    behind = dot_sum(lower.astype(F32), grad_cum, TN) + dot_sum(at_end, hot)[:1, :]
    grad_step = behind * log_rate + dot_sum(dx_prod, hot)
    grad_dt = grad_step * sigmoid(dt_val)
    ddt_ref[...] = grad_dt.astype(BF16)
    skip_sum = jnp.broadcast_to(jnp.sum(dy_x, axis=0, keepdims=True), (EDGE, inner))
    row = lax.broadcasted_iota(jnp.int32, (EDGE, LANES), 0)
    heads_out_ref[...] = jnp.where(
        row == 0,
        jnp.sum(grad_dt, axis=0, keepdims=True),
        jnp.where(
            row == 1,
            jnp.sum(step * behind, axis=0, keepdims=True) * log_rate,
            jnp.where(row == 2, dot_sum(skip_sum, hot), 0.0),
        ),
    )
    grad_conv = jnp.concatenate([grad_x, grad_b, grad_c], axis=1) * (
        sig * (1.0 + conv * (1.0 - sig))
    )
    channels = conv.shape[1]
    line_ref[: 2 * EDGE, :] = jnp.zeros((2 * EDGE, channels), F32)
    line_ref[2 * EDGE : 2 * EDGE + tokens, :] = grad_conv
    line_ref[2 * EDGE + tokens :, :] = jnp.zeros((EDGE, channels), F32)
    mixed = jnp.zeros((tokens + EDGE, channels), F32)
    for tap in range(CONV):
        first = EDGE + CONV - 1 - tap
        mixed = mixed + taps_ref[tap : tap + 1, :] * line_ref[first : first + tokens + EDGE, :]
        first = EDGE - CONV + 1 + tap
        small_ref[tap : tap + 1, :] = jnp.sum(
            grad_conv * pad_ref[first : first + tokens, :], axis=0, keepdims=True
        )
    small_ref[CONV : CONV + 1, :] = jnp.sum(grad_conv, axis=0, keepdims=True)
    small_ref[CONV + 1 :, :] = jnp.zeros((EDGE - CONV - 1, channels), F32)
    mixed_ref[...] = mixed


def normed_back(
    where_ref, mixed_ref, next_ref, small_ref, dz_ref, ddt_ref, zx_ref, bc_ref, dt_ref,
    x_low_ref, bc_out_ref, keep_ref, send_ref, whole_ref
):
    tokens = mixed_ref.shape[0] - EDGE
    inner = dz_ref.shape[1]
    fill = jnp.zeros((tokens - EDGE, mixed_ref.shape[1]), F32)
    mixed = mixed_ref[EDGE:, :] + jnp.concatenate([fill, next_ref[...]], axis=0)
    x_low = mixed[:, :inner].astype(BF16)
    x_low_ref[...] = x_low
    grad_bc = mixed[:, inner:]
    bc_out_ref[:tokens, :] = grad_bc
    bc_out_ref[tokens:, :] = small_ref[:, inner:]
    high, rest = halves(grad_bc)
    total = (
        dot_low(dz_ref[...], zx_ref[:, :inner], NT)
        + dot_low(x_low, zx_ref[:, inner:], NT)
        + dot_low(high, bc_ref[...], NT)
        + dot_low(rest, bc_ref[...], NT)
        + dot_low(ddt_ref[...], dt_ref[...], NT)
    )
    whole_ref[...] = total
    deal_rows(where_ref, whole_ref, keep_ref, send_ref)


def input_back(where_ref, grad_ref, in_ref, gain_ref, *refs):
    *terms, out_ref, sum_ref, kept_ref = refs
    total = stacked(*terms)
    rows = total.shape[0]

    def half(ref):
        value = ref[half_at(where_ref, 0, rows), :] if ref.shape[0] > rows else ref[...]
        return value.astype(F32)

    block_in = half(in_ref)
    scale = lax.rsqrt(jnp.mean(block_in * block_in, axis=-1, keepdims=True) + EPS)
    weighted = total * gain_ref[...]
    inner_prod = jnp.mean(weighted * block_in, axis=-1, keepdims=True)
    out_ref[...] = (
        half(grad_ref) + scale * weighted - block_in * (scale * scale * scale * inner_prod)
    )
    kept_ref[...] = out_ref[...]
    sum_ref[...] = jnp.broadcast_to(
        jnp.sum(total * block_in * scale, axis=0, keepdims=True), sum_ref.shape
    )


def split_bc(own_ref, got_ref, keep_ref, send_ref):
    total = own_ref[...] + got_ref[...]
    quarter = total.shape[1] // 4
    cols = [total[:, at * quarter : (at + 1) * quarter] for at in range(4)]
    keep_ref[...] = jnp.concatenate([cols[0], cols[2]], axis=1)
    send_ref[...] = jnp.concatenate([cols[1], cols[3]], axis=1)


def narrow_bc(own_ref, got_ref, keep_ref, send_ref):
    total = own_ref[...] + got_ref[...]
    quarter = total.shape[1] // 4
    cols = [total[:, at * quarter : (at + 1) * quarter] for at in range(4)]
    fill = jnp.zeros((total.shape[0], 2 * quarter), F32)
    keep_ref[...] = jnp.concatenate([cols[0], cols[2], fill], axis=1)
    send_ref[...] = jnp.concatenate([cols[1], cols[3], fill], axis=1)


def x_grads(where_ref, n0_ref, n1_ref, x0_ref, x1_ref, keep_ref, send_ref, out_ref, *, rows):
    out_ref[...] = dot_low(n0_ref[...], x0_ref[...], TN) + dot_low(n1_ref[...], x1_ref[...], TN)
    deal_chunks(where_ref, rows, 0, lambda span: out_ref[span, :], keep_ref, send_ref)


def narrow_grads(
    where_ref, half_ref, got_ref, n0_ref, n1_ref, d0_ref, d1_ref, keep_ref, send_ref, rows_ref,
    out_ref, *, pair, rows
):
    total = half_ref[...] + got_ref[...]
    tokens = n0_ref.shape[0]
    low = total[:tokens].astype(BF16)
    rows_ref[...] = total[tokens:]
    normed = jnp.where(where_ref[0] == 0, n0_ref[...].astype(F32), n1_ref[...].astype(F32))
    bc = dot_low(normed, low, TN)
    dt = dot_low(n0_ref[...], d0_ref[...], TN) + dot_low(n1_ref[...], d1_ref[...], TN)
    out_ref[...] = jnp.concatenate([bc[:, :pair], dt[:, : LANES - pair]], axis=1)
    deal_chunks(where_ref, rows, 0, lambda span: out_ref[span, :], keep_ref, send_ref)


def early_grads(
    where_ref, n0_ref, n1_ref, z0_ref, z1_ref, g0_ref, g1_ref, o0_ref, o1_ref, keep_ref, send_ref,
    out_ref, *, rows
):
    inner = z0_ref.shape[1]
    out_ref[:, :inner] = dot_low(n0_ref[...], z0_ref[...], TN) + dot_low(
        n1_ref[...], z1_ref[...], TN
    )
    out_ref[:, inner:] = dot_low(g0_ref[...], o0_ref[...], TN) + dot_low(
        g1_ref[...], o1_ref[...], TN
    )
    deal_chunks(where_ref, rows, 0, lambda span: out_ref[span, :], keep_ref, send_ref)


def sum_rows(bc_ref, *refs, micro):
    small, heads, grow, gains = (refs[at * micro : (at + 1) * micro] for at in range(4))
    out_ref = refs[-1]
    inner = grow[0].shape[1]

    def total(values):
        return functools.reduce(jnp.add, [one[...] for one in values])

    out_ref[...] = jnp.zeros(out_ref.shape, F32)
    out_ref[:EDGE, :inner] = total(small)[:, :inner]
    out_ref[CONV + 1 : CONV + 2, :inner] = total(grow)[:1]
    out_ref[EDGE : 2 * EDGE, :LANES] = total(heads)
    out_ref[EDGE : 2 * EDGE, LANES : 2 * LANES] = bc_ref[...]
    out_ref[CONV + 2 : CONV + 3, :] = total(gains)[:1]


def choose_ends(where_ref, *refs):
    *pieces, send_ref, keep_ref = refs
    micro = len(pieces) // 2
    lower, upper = pieces[:micro], pieces[micro:]

    def write(target_ref, sources):
        for index in range(micro):
            target_ref[index] = sources[index][...]

    @pl.when(where_ref[0] == 0)
    def _():
        write(keep_ref, lower)
        write(send_ref, upper)

    @pl.when(where_ref[0] != 0)
    def _():
        write(keep_ref, upper)
        write(send_ref, lower)


def lay_out(where_ref, own_ref, got_ref, out_ref):
    rows = own_ref.shape[1]
    for index in range(own_ref.shape[0]):
        out_ref[index, half_at(where_ref, 0, rows), :] = own_ref[index]
        out_ref[index, half_at(where_ref, 1, rows), :] = got_ref[index]


def swap(block):
    return lax.ppermute(block, "section", [(0, 1), (1, 0)])


def across(block, mask):
    count = lax.axis_size("head")
    return lax.ppermute(block, "head", [(i, i ^ mask) for i in range(count)])


def along(block, distance):
    devices = range(lax.axis_size("seq"))
    return lax.ppermute(
        block, "seq", [(i, i + distance) for i in devices if i + distance in devices]
    )


def fused(body, *args):
    return kernel_call(body, [(args[0].shape, F32)], args, 0.5, scalars=False)[0]


def carried(own, direction):
    count = lax.axis_size("seq")
    near = along(own, direction)
    yield
    far = jnp.zeros_like(near)
    distance = 2
    while distance < count:
        window = fused(join_window, own, near)
        far = along(window, direction * distance)
        yield
        distance *= 2
        if distance < count:
            near = fused(join_window, near, far)
    return near, far


def sum_all(value):
    got = swap(value)
    yield
    value = fused(add_pair, value, got)
    near, side, far = (across(value, mask) for mask in (1, 2, 3))
    yield
    return fused(add_pair, value, near), fused(add_pair, side, far)


def sum_halves(keep, send):
    got = swap(send)
    yield
    shape = (keep.shape[0] // 2, keep.shape[1])
    first, second = kernel_call(
        add_split, [(shape, F32)] * 2, (keep, got), 0.5, scalars=False
    )
    got_first, got_second = across(first, 1), across(second, 2)
    yield
    first = fused(add_pair, first, got_first)
    got_first = across(first, 2)
    second = fused(add_pair, second, got_second)
    got_second = across(second, 1)
    yield
    return first, got_first, second, got_second


def sum_seq(value):
    count = lax.axis_size("seq")
    got = jnp.zeros_like(value)
    mask = 1
    while mask < count:
        if mask > 1:
            value = fused(add_pair, value, got)
        got = lax.ppermute(value, "seq", [(i, i ^ mask) for i in range(count)])
        yield
        mask *= 2
    return value, got


def on_device(
    inputs, cotangent, in_gain, w_z, w_x, w_bc, w_dt, dt_bias, a_log, skip, conv_x, conv_bc,
    convb_x, convb_bc, norm_gain, w_out
):
    section = lax.axis_index("section")
    parts = lax.axis_size("head")
    where = jnp.stack([section, lax.axis_index("seq")]).astype(jnp.int32)
    micro, tokens, model_w = inputs.shape
    inner = w_z.shape[2] // 2
    heads_n = w_dt.shape[2] // 2
    state_loc = w_bc.shape[3]
    pair = 2 * state_loc
    state_w = state_loc * parts
    channels = inner + 2 * state_w
    rows = tokens // 2
    half = model_w // 2

    pack, send_zx, send_out, own_rows, edge_in = kernel_call(
        pack_weights,
        [((half + EDGE, 2 * pair), F32), ((model_w, 2 * inner), F32), ((inner, model_w), F32),
         ((3 * EDGE, model_w), F32), ((micro, EDGE, model_w), F32)],
        (where, Kept(inputs), Kept(w_z[0]), Kept(w_x[0]), Kept(w_out[0]), Kept(w_bc[0].reshape(model_w, pair)),
         *[
             Kept(one)
             for one in (
                 conv_bc[0].reshape(CONV, pair), convb_bc.reshape(1, pair), w_dt[0], conv_x[0],
                 convb_x, norm_gain, in_gain, dt_bias, a_log, skip,
             )
         ]),
        3, held=True,
    )
    own_packs = [pack] + [across(pack, part) for part in range(1, parts)]
    got_rows = swap(own_rows)
    got_zx = swap(send_zx)
    got_out = swap(send_out)
    halo_in = along(edge_in, 1)
    got_packs = [swap(one) for one in own_packs]
    def weight_outs(*more):
        return [
            ((model_w, 2 * inner), BF16, *more), ((model_w, 2 * state_w), BF16, *more),
            ((model_w, LANES), BF16, *more), ((inner, model_w), BF16, *more),
            ((EDGE, channels), F32, *more), ((EDGE, LANES), F32, *more),
            ((1, inner), F32, *more), ((1, model_w), F32, *more),
        ]

    picked = kernel_call(
        functools.partial(pick_weights, parts=parts),
        weight_outs(True) + weight_outs(True) + weight_outs(),
        (where, Kept(w_z[0]), Kept(w_x[0]), Kept(w_out[0]), got_zx, got_out, own_rows, got_rows,
         *own_packs, *got_packs),
        4,
    )
    blocks = (picked[:8], picked[8:16])
    w_zxs, w_bcs, w_dts, w_outs, taps, head_rows, gains, in_gains = zip(*blocks)
    now = picked[16:]

    project_outs = [
        ((tokens, model_w), BF16, True),
        ((tokens, inner), F32, True),
        ((tokens + EDGE, channels), F32, True),
        ((tokens, channels), F32, True),
        ((tokens, LANES), F32, True),
        ((tokens, LANES), F32, True),
        ((state_w + EDGE, inner), F32, True),
        ((tokens, inner), F32),
        ((tokens, state_w), F32),
        ((tokens, inner), F32),
        ((tokens, inner), F32),
        ((state_w + EDGE, inner), F32),
    ]
    halves_out = [((rows, model_w), F32)] * 2
    whole_scratch = [pltpu.VMEM((tokens, model_w), F32)]

    def summed(sums):
        return fused(add_pair, *sum_heads(fused(add_pair, sums, swap(sums)), 1))

    def forward_first(index):
        *kept, gate, c_ssd, grown, local, state = kernel_call(
            first_forward, project_outs,
            (Kept(inputs, index), halo_in[index], now[7], *now[:3], now[4], now[5]),
            3, scalars=False,
        )
        near, far = yield from carried(state, 1)
        ssd, entry, gated, sums = kernel_call(
            first_output,
            [((tokens, inner), F32, True), ((state_w, inner), F32, True), ((tokens, inner), F32),
             ((EDGE, tokens), F32)],
            (local, near, far, c_ssd, grown, gate), 1, scalars=False,
        )
        sums = yield from sum_all(sums)
        _, keep, send, sums = kernel_call(
            first_branch,
            [((tokens, inner), BF16, True)] + halves_out + [((EDGE, tokens), F32, True)],
            (where, *sums, gated, now[6], now[3]), 2, scratch=whole_scratch,
        )
        terms = yield from sum_halves(keep, send)
        own, own_kept = kernel_call(
            add_base, [((rows, model_w), F32), ((rows, model_w), F32, True)],
            (where, Kept(inputs, index), *terms), 1,
        )
        return (*kept, entry, ssd), own, sums, own_kept

    def forward_second(index, own):
        other = swap(own)
        top = jnp.where(section == 0, other[rows - EDGE :], own[rows - EDGE :])
        halo = along(top, 1)
        yield
        block_in, *kept, gate, c_ssd, grown, local, state = kernel_call(
            later_forward, [((tokens, model_w), F32, True)] + project_outs,
            (where, own, other, halo, in_gains[1], w_zxs[1], w_bcs[1], w_dts[1], taps[1],
             head_rows[1]),
            4,
        )
        near, far = yield from carried(state, 1)
        ssd, entry, grad_norm, sums = kernel_call(
            second_output,
            [((tokens, inner), F32, True), ((state_w, inner), F32, True), ((tokens, inner), F32),
             ((EDGE, tokens), F32)],
            (local, near, far, c_ssd, grown, gate, gains[1], w_outs[1], Kept(cotangent, index)),
            2, scalars=False,
        )
        sums = yield from sum_all(sums)
        return (*kept, entry, ssd), block_in, grad_norm, sums

    gate_outs = [
        ((tokens, inner), F32),
        ((tokens, inner), BF16, True),
        ((tokens, inner), BF16, True),
        ((EDGE, inner), F32, True),
        ((state_w + EDGE, inner), F32),
    ]

    def back_rest(block, kept, dy, dz, grad_entry):
        _, _, pad, conv, dt_val, cum, state, entry, ssd = kept
        near, far = yield from carried(grad_entry, -1)
        mixed, ddt, small, head_sums = kernel_call(
            scan_back,
            [((tokens + EDGE, channels), F32), ((tokens, LANES), BF16, True),
             ((EDGE, channels), F32, True), ((EDGE, LANES), F32, True)],
            (dy, ssd, conv, pad, dt_val, cum, entry, state, near, far, taps[block],
             head_rows[block]),
            4, scratch=[pltpu.VMEM((tokens + 3 * EDGE, channels), F32)], scalars=False, held=True,
        )
        from_next = along(mixed[:EDGE], -1)
        yield
        x_low, grad_bc, keep, send = kernel_call(
            normed_back,
            [((tokens, inner), BF16, True), ((tokens + EDGE, 2 * state_w), F32)] + halves_out,
            (where, mixed, from_next, small, dz, ddt, w_zxs[block], w_bcs[block], w_dts[block]),
            2, scratch=whole_scratch,
        )
        return (x_low, ddt, grad_bc, small, head_sums), keep, send

    def input_grad(block, grad_half, in_half, *terms):
        return kernel_call(
            input_back,
            [((rows, model_w), F32), ((EDGE, model_w), F32, True), ((rows, model_w), F32, True)],
            (where, grad_half, in_half, in_gains[block], *terms), 1,
        )

    shards = lax.axis_size("seq")
    chunk = model_w // shards

    def scattered(keep, send):
        step = 1
        while True:
            mask = 1 << (step - 1)
            pairs = [(i, i ^ mask) for i in range(shards)]
            got = lax.ppermute(send, "seq", pairs)
            yield
            if 2 * mask >= shards:
                return keep, got
            shape = (keep.shape[0] // 2, keep.shape[1])
            keep, send = kernel_call(
                functools.partial(add_chunks, rows=chunk, step=step), [(shape, F32)] * 2,
                (where, keep, got), 0.5,
            )
            step += 1

    def dealt(width):
        return [((model_w // 2, width), F32)] * 2

    def first_grads(normed_all, gates, grads):
        keep, send = kernel_call(
            functools.partial(early_grads, rows=chunk), dealt(2 * inner),
            (where, *normed_all, *[one[1] for one in gates], *grads, *[one[2] for one in gates]),
            3, scratch=[pltpu.VMEM((model_w, 2 * inner), F32)],
        )
        return (yield from scattered(keep, send))

    def second_grads(normed_all, rests):
        keep, send = kernel_call(
            functools.partial(x_grads, rows=chunk), dealt(inner),
            (where, *normed_all, *[one[0] for one in rests]),
            2, scratch=[pltpu.VMEM((model_w, inner), F32)],
        )
        return (yield from scattered(keep, send))

    def third_grads(normed_all, rests, block):
        ddt, grad_bc = ([one[at] for one in rests] for at in (1, 2))
        shape = (grad_bc[0].shape, F32)
        own, other = kernel_call(pick_pair, [shape] * 2, (where, *grad_bc), 0.5)
        got = swap(other)
        yield
        thin = [((tokens + EDGE, 2 * pair), F32)] * 2
        keep, send = kernel_call(split_bc, thin, (own, got), 0.5, scalars=False)
        got = across(send, 1)
        yield
        keep, send = kernel_call(narrow_bc, thin, (keep, got), 0.5, scalars=False)
        got = across(send, 2)
        yield
        keep, send, bc_rows = kernel_call(
            functools.partial(narrow_grads, pair=pair, rows=chunk),
            dealt(LANES) + [((EDGE, LANES), F32, True)],
            (where, keep, got, *normed_all, *ddt), 2,
            scratch=[pltpu.VMEM((model_w, LANES), F32)],
        )
        found["bc", block] = bc_rows
        return (yield from scattered(keep, send))

    def row_sums(bc_rows, rests, grow_all, gain_all):
        (total,) = kernel_call(
            functools.partial(sum_rows, micro=micro), [((2 * EDGE, model_w), F32)],
            (bc_rows, *[one[3] for one in rests], *[one[4] for one in rests], *grow_all,
             *gain_all),
            0.5, scalars=False,
        )
        return (yield from sum_seq(total))

    each = range(micro)
    both = tuple("m%d" % index for index in each)
    first = [None] * micro
    second = [None] * micro
    gates = [[None] * micro, [None] * micro]
    rests = [[None] * micro, [None] * micro]
    mids = [None] * micro
    lasts = [None] * micro
    upper = [None] * micro
    lows = [None] * micro

    def chain(index):
        first[index] = yield from forward_first(index)
        second[index] = yield from forward_second(index, first[index][1])
        kept, block_in, grad_norm, sums = second[index]
        gates[1][index] = kernel_call(
            second_gate, gate_outs,
            (*sums, grad_norm, kept[8], kept[1], gains[1], kept[3], kept[5], kept[6]),
            2, scalars=False,
        )
        dy, dz, _, _, grad_entry = gates[1][index]
        rests[1][index], keep, send = yield from back_rest(1, kept, dy, dz, grad_entry)
        terms = yield from sum_halves(keep, send)
        mids[index] = input_grad(1, Kept(cotangent, index), first[index][3], *terms)
        own = mids[index][0]
        other = swap(own)
        yield
        kept = first[index][0]
        lows[index], *gates[0][index] = kernel_call(
            first_gate, [((tokens, model_w), BF16, True)] + gate_outs,
            (where, own, other, block_in, Kept(inputs, index), first[index][2], w_outs[0],
             kept[8], kept[1], gains[0], kept[3], kept[5], kept[6]),
            3, scratch=whole_scratch,
        )
        dy, dz, _, _, grad_entry = gates[0][index]
        rests[0][index], keep, send = yield from back_rest(0, kept, dy, dz, grad_entry)
        terms = yield from sum_halves(keep, send)
        lasts[index] = input_grad(0, mids[index][2], Kept(inputs, index), *terms)

    def top_output(index):
        until(full(gates[1]), *both)
        keep, send = kernel_call(
            out_project, halves_out, (where, gates[1][index][2], w_outs[1]), 1,
            scratch=whole_scratch,
        )
        terms = yield from sum_halves(keep, send)
        upper[index] = kernel_call(
            add_base, [((rows, model_w), F32, True)] * 2, (where, first[index][3], *terms), 1
        )

    found = {}

    def normed_of(block):
        return [one[0][0] for one in (first, second)[block]]

    def until(ready, *names):
        while not ready():
            for name in names:
                next(chains[name], None)

    def full(values):
        return lambda: all(value is not None for value in values)

    def part(name, block):
        if name == "early":
            until(full(gates[block]), *both)
        elif name == "rows":
            until(lambda: ("bc", block) in found, "narrow%d" % block)
            until(full((lasts, mids)[block]), *both)
        else:
            until(full(rests[block]), *both)
        if name == "early":
            grads = lows if block == 0 else [Kept(cotangent, index) for index in each]
            found[name, block] = yield from first_grads(normed_of(block), gates[block], grads)
        elif name == "wide":
            found[name, block] = yield from second_grads(normed_of(block), rests[block])
        elif name == "narrow":
            found[name, block] = yield from third_grads(
                normed_of(block), rests[block], block
            )
        else:
            gain_all = [one[1] for one in (lasts, mids)[block]]
            found[name, block] = yield from row_sums(
                found["bc", block], rests[block], [one[3] for one in gates[block]],
                gain_all,
            )

    def trade(name):
        if name == "ends":
            until(full(lasts), *both)
            until(full(upper), "u0", "u%d" % (micro - 1))
            shape = (micro, rows, model_w)
            send, keep = kernel_call(
                choose_ends, [(shape, F32), (shape, F32)],
                (where, *[one[0] for one in lasts], *[one[0] for one in upper]), 1,
            )
        else:
            for block in (0, 1):
                until(lambda: (name, block) in found, "%s%d" % (name, block))
            low_one, top_one = found[name, 0], found[name, 1]
            shape = low_one[0].shape
            keep, send = kernel_call(
                pick_sums, [(shape, F32), (shape, F32)], (where, *low_one, *top_one), 0.5
            )
        found["trade", name] = keep, swap(send)
        yield

    chains = {"m%d" % index: chain(index) for index in each}
    chains.update({"u%d" % index: top_output(index) for index in each})
    chains.update({"t" + name: trade(name) for name in ("early", "wide", "narrow", "rows", "ends")})
    for block in (0, 1):
        for name in ("early", "wide", "narrow", "rows"):
            chains["%s%d" % (name, block)] = part(name, block)

    def run(*names):
        for name in names:
            next(chains[name], None)

    while gates[1][-1] is None:
        run(*both)
    a, b = both[0], both[-1]
    for names in SCHEDULE:
        run(*[{"a": a, "b": b}.get(name, name) for name in names])
    for name in ("tearly", "twide", "tnarrow", "trows", "tends"):
        for _ in chains[name]:
            pass
    (ends,) = kernel_call(
        lay_out, [((micro, tokens, model_w), F32, True)], (where, *found["trade", "ends"]), 1
    )
    size = chunk
    own, got = found["trade", "early"]
    g_w_z, g_w_out = kernel_call(
        join_first, [((size, 2 * inner), F32, True), ((2 * inner, size), F32, True)],
        (where, own, got), 1,
    )
    own, got = found["trade", "wide"]
    (g_w_x,) = kernel_call(join_second, [((size, 2 * inner), F32, True)], (where, own, got), 1)
    own, got = found["trade", "narrow"]
    narrow, own_dt, got_dt = own + got, own, got
    g_w_bc = narrow[:, :pair].reshape(-1, 2, state_loc)
    mine = section == 0

    def both_sides(own, got):
        return jnp.concatenate([jnp.where(mine, own, got), jnp.where(mine, got, own)], axis=1)

    g_w_dt = both_sides(own_dt[:, pair : pair + heads_n], got_dt[:, pair : pair + heads_n])
    own, got = found["trade", "rows"]
    shapes = [
        (CONV, 2 * inner), (1, 2 * inner), (1, 2 * inner), (1, model_w), (1, 2 * heads_n),
        (1, 2 * heads_n), (1, 2 * heads_n), (EDGE, pair),
    ]
    *row_set, bc_set = (
        one.value
        for one in kernel_call(
            join_rows, [(shape, F32, True) for shape in shapes], (where, own, got), 0.5
        )
    )
    g_conv_x, g_convb_x, g_norm_gain, g_in_gain, g_bias, g_log, g_skip = row_set
    return (
        ends.value[None],
        g_in_gain,
        g_w_z.value[None],
        g_w_x.value[None],
        g_w_bc[None],
        g_w_dt[None],
        g_bias,
        g_log,
        g_skip,
        g_conv_x[None],
        bc_set[:CONV].reshape(1, CONV, 2, state_loc),
        g_convb_x,
        bc_set[CONV : CONV + 1].reshape(1, 2, state_loc),
        g_norm_gain,
        g_w_out.value[None],
    )


def solution(mesh):
    Line.mark = None
    in_specs = (
        P(None, "seq", None),
        P(None, "seq", None),
        P("section", None),
        P("section", None, "head"),
        P("section", None, "head"),
        P("section", None, None, "head"),
        P("section", None, "head"),
        P("section", "head"),
        P("section", "head"),
        P("section", "head"),
        P("section", None, "head"),
        P("section", None, None, "head"),
        P("section", "head"),
        P("section", None, "head"),
        P("section", "head"),
        P("section", "head", None),
    )
    out_specs = (
        P("section", None, "seq", None),
        P("section", None),
        P("section", "seq", "head"),
        P("section", "seq", "head"),
        P("section", "seq", None, "head"),
        P("section", "seq", "head"),
        P("section", "head"),
        P("section", "head"),
        P("section", "head"),
        P("section", None, "head"),
        P("section", None, None, "head"),
        P("section", "head"),
        P("section", None, "head"),
        P("section", "head"),
        P("section", "head", "seq"),
    )
    return jax.shard_map(
        on_device, mesh=mesh, in_specs=in_specs, out_specs=out_specs, check_vma=False
    )
```
